256 devices in a mesh: group: 16 (over z_lo, y, core), tensor: 16 (over z_hi, x).
Axes of the slice: x: 4, y: 4, z: 8 (z_hi: 4, z_lo: 2; z = z_hi * 2 + z_lo), core: 2. Of those that a mesh axis runs over, the one named last changes fastest.
Arguments:
- hidden: bfloat16 [1536, 4608], P('group', 'tensor'), may hold values from -6 to 6
- cache_len: int32 [1536], P('group'), may hold values from 1 to 96, as said below
- layer_index: int32 [1], replicated, may hold values from 0 to 15
- pre_gain: float32 [4608], replicated, may hold values from 0.1 to 1.9
- post_gain: float32 [4608], replicated, may hold values from 0.1 to 1.9
- w_query: bfloat16 [4608, 4096], P(None, 'tensor'), may hold values from -0.09375 to 0.09375
- w_key: bfloat16 [4608, 2048], P(None, 'tensor'), may hold values from -0.09375 to 0.09375
- w_value: bfloat16 [4608, 2048], P(None, 'tensor'), may hold values from -0.09375 to 0.09375
- w_out: bfloat16 [4096, 4608], P('tensor'), may hold values from -0.09375 to 0.09375
- cache_keys: bfloat16 [1536, 96, 2048], P('group', None, 'tensor'), may hold values from -6 to 6
- cache_values: bfloat16 [1536, 96, 2048], P('group', None, 'tensor'), may hold values from -6 to 6
- wide_factors: float32 [16, 2, 64, 4608], P('group', None, None, 'tensor')
- narrow_factors: float32 [16, 2, 64, 4096], P('group', None, None, 'tensor')
- wide_momentum: float32 [16, 2, 64, 4608], P('group', None, None, 'tensor')
- narrow_momentum: float32 [16, 2, 64, 4096], P('group', None, None, 'tensor')
- wide_gradient: float32 [16, 2, 64, 4608], P('group', None, None, 'tensor')
- narrow_gradient: float32 [16, 2, 64, 4096], P('group', None, None, 'tensor')
Outputs:
- hidden_out: bfloat16 [1536, 4608], P('group', 'tensor')
The draws below stay inside these ranges and needn't reach their ends.
Inputs may be any that keep to these rules, and one draw needn't show every extreme that they name: `cache_len`: in every group's block of 96 rows the first row has all 96 slots filled.
All inputs are finite; a program needn't handle non-finite values.
Results may differ from the reference program's by a relative error of at most 0.02.
Values may be sent and summed in bfloat16 or wider, within the bound.
No kernel may reach another device: no remote copies, remote signals or barrier semaphores. Data moves between devices by JAX's collectives and lax.ppermute only.
A program may use at most 128 MiB of HBM per device.

```python
import jax
import jax.numpy as jnp
from jax import lax

D = 4608
HQ = 32
HD = 128
R = 64
ROWS = 96
CACHE = 96
STEPS = 4
QW = 4096
KVW = 2048
ROWS_ALL = 1536
LAYERS = 16


def scaled_pair(sample, first_scale, second_scale):
    factors = jnp.array([first_scale, second_scale], jnp.float32).reshape(1, 2, 1, 1)
    return sample * factors


def draw_cache_len(key, part):
    key = jax.random.fold_in(key, 5)
    lengths = jax.random.randint(key, (ROWS_ALL,), 1, CACHE + 1)
    return lengths.at[::ROWS].set(CACHE).astype(jnp.int32)


def draw_wide_factors(key, part):
    key = jax.random.fold_in(key, 11)
    full_shape = (LAYERS, 2, R, D)
    sample = jax.random.normal(key, full_shape, jnp.float32)
    return scaled_pair(sample, D ** (-0.5), R ** (-0.5))


def draw_narrow_factors(key, part):
    key = jax.random.fold_in(key, 12)
    full_shape = (LAYERS, 2, R, QW)
    sample = jax.random.normal(key, full_shape, jnp.float32)
    return scaled_pair(sample, R ** (-0.5), QW ** (-0.5))


def draw_wide_momentum(key, part):
    key = jax.random.fold_in(key, 13)
    full_shape = (LAYERS, 2, R, D)
    sample = jax.random.normal(key, full_shape, jnp.float32)
    return scaled_pair(sample, D ** (-0.5), R ** (-0.5))


def draw_narrow_momentum(key, part):
    key = jax.random.fold_in(key, 14)
    full_shape = (LAYERS, 2, R, QW)
    sample = jax.random.normal(key, full_shape, jnp.float32)
    return scaled_pair(sample, R ** (-0.5), QW ** (-0.5))


def draw_wide_gradient(key, part):
    key = jax.random.fold_in(key, 15)
    full_shape = (LAYERS, 2, R, D)
    sample = jax.random.normal(key, full_shape, jnp.float32)
    return scaled_pair(sample, D ** (-0.5), R ** (-0.5))


def draw_narrow_gradient(key, part):
    key = jax.random.fold_in(key, 16)
    full_shape = (LAYERS, 2, R, QW)
    sample = jax.random.normal(key, full_shape, jnp.float32)
    return scaled_pair(sample, R ** (-0.5), QW ** (-0.5))


def steps_of(own_key, extent, shards, least, high):
    factor_of, own = 1.0, jax.random.fold_in(own_key, 6)
    for axis_at, shards_of in shards:
        heights = jnp.exp(jax.random.uniform(jax.random.fold_in(own, axis_at), (shards_of,), jnp.float32, least / len(shards), high / len(shards)))
        factor_of = factor_of * jnp.repeat(heights, extent[axis_at] // shards_of).reshape([-1 if axis == axis_at else 1 for axis in range(len(extent))])
    return factor_of


def normal_values(stream_key, dims, scale, most, cuts=(), kind=jnp.bfloat16):
    gain = steps_of(stream_key, dims, cuts, -0.22, 0.18) if cuts else 1.0
    values = jax.random.normal(stream_key, dims, jnp.float32) * scale * gain
    return jnp.minimum(jnp.maximum(values, -most), most).astype(kind)


def setup_inputs(seed: int = 0) -> dict:
    key_list = jax.random.split(jax.random.key(seed), 18)
    hidden = normal_values(key_list[0], (ROWS_ALL, D), 1.0, 6.0, ((0, 16), (1, 16)))
    cache_len = draw_cache_len(jax.random.fold_in(key_list[17], 71), 0)
    layer_index = jax.random.randint(key_list[2], (1,), 0, LAYERS).astype(jnp.int32)
    pre_gain = jnp.clip(1.0 + 0.18 * jax.random.normal(key_list[3], (D,), jnp.float32), 0.1, 1.9)
    post_gain = jnp.clip(1.0 + 0.18 * jax.random.normal(key_list[4], (D,), jnp.float32), 0.1, 1.9)
    w_query = normal_values(key_list[5], (D, QW), D ** -0.5, 0.09375, ((1, 16),))
    w_key = normal_values(key_list[6], (D, KVW), D ** -0.5, 0.09375, ((1, 16),))
    w_value = normal_values(key_list[7], (D, KVW), D ** -0.5, 0.09375, ((1, 16),))
    w_out = normal_values(key_list[8], (QW, D), QW ** -0.5, 0.09375, ((0, 16),))
    cache_keys = normal_values(key_list[9], (ROWS_ALL, CACHE, KVW), 1.0, 6.0, ((0, 16), (2, 16)))
    cache_values = normal_values(key_list[10], (ROWS_ALL, CACHE, KVW), 1.0, 6.0, ((0, 16), (2, 16)))
    wide_factors = draw_wide_factors(jax.random.fold_in(key_list[17], 71), 0)
    narrow_factors = draw_narrow_factors(jax.random.fold_in(key_list[17], 71), 0)
    wide_momentum = draw_wide_momentum(jax.random.fold_in(key_list[17], 71), 0)
    narrow_momentum = draw_narrow_momentum(jax.random.fold_in(key_list[17], 71), 0)
    wide_gradient = draw_wide_gradient(jax.random.fold_in(key_list[17], 71), 0)
    narrow_gradient = draw_narrow_gradient(jax.random.fold_in(key_list[17], 71), 0)
    return dict(hidden=hidden, cache_len=cache_len, layer_index=layer_index, pre_gain=pre_gain, post_gain=post_gain, w_query=w_query, w_key=w_key, w_value=w_value, w_out=w_out, cache_keys=cache_keys, cache_values=cache_values, wide_factors=wide_factors, narrow_factors=narrow_factors, wide_momentum=wide_momentum, narrow_momentum=narrow_momentum, wide_gradient=wide_gradient, narrow_gradient=narrow_gradient)


LEARN_RATE = 0.25
MOMENTUM_DECAY = 0.9
EPSILON = 1e-06
SOFT_CAP = 50.0
ROPE_BASE = 10000.0

def rotate(matrix, position):
    head_count = matrix.shape[1] // HD
    half_width = HD // 2
    frequency = ROPE_BASE ** (-jnp.arange(half_width, dtype=jnp.float32) * 2.0 / HD)
    angles = position[:, None] * frequency[None, :]
    cosine_table = jnp.cos(angles)[:, None, :]
    sine_table = jnp.sin(angles)[:, None, :]
    pieces = matrix.reshape(matrix.shape[0], head_count, HD)
    first_half = pieces[..., :half_width]
    second_half = pieces[..., half_width:]
    turned = jnp.concatenate([first_half * cosine_table - second_half * sine_table, second_half * cosine_table + first_half * sine_table], axis=-1)
    return turned.reshape(matrix.shape[0], head_count * HD)

def attend(queries, old_keys, old_values, fresh_keys, fresh_values, lengths, turn_index):
    row_count = queries.shape[0]
    kv_heads = old_keys.shape[2] // HD
    group_size = queries.shape[1] // old_keys.shape[2]
    cache_slots = old_keys.shape[1]
    fresh_slots = fresh_keys.shape[1]
    score_scale = (D / HQ) ** (-0.5)
    query_heads = queries.astype(jnp.float32).reshape(row_count, kv_heads, group_size, HD)
    cache_k = old_keys.astype(jnp.float32).reshape(row_count, cache_slots, kv_heads, HD)
    cache_v = old_values.astype(jnp.float32).reshape(row_count, cache_slots, kv_heads, HD)
    recent_k = fresh_keys.astype(jnp.float32).reshape(row_count, fresh_slots, kv_heads, HD)
    recent_v = fresh_values.astype(jnp.float32).reshape(row_count, fresh_slots, kv_heads, HD)
    cache_scores = jnp.einsum('rkgd,rckd->rkgc', query_heads, cache_k) * score_scale
    recent_scores = jnp.einsum('rkgd,rskd->rkgs', query_heads, recent_k) * score_scale
    cache_scores = SOFT_CAP * jnp.tanh(cache_scores / SOFT_CAP)
    recent_scores = SOFT_CAP * jnp.tanh(recent_scores / SOFT_CAP)
    cache_mask = jnp.arange(cache_slots)[None, :] < lengths[:, None]
    recent_mask = jnp.arange(fresh_slots) <= turn_index
    cache_exp = jnp.where(cache_mask[:, None, None, :], jnp.exp(cache_scores), 0.0)
    recent_exp = jnp.where(recent_mask[None, None, None, :], jnp.exp(recent_scores), 0.0)
    denominator = lax.optimization_barrier(jnp.sum(cache_exp, axis=-1, keepdims=True)) + lax.optimization_barrier(jnp.sum(recent_exp, axis=-1, keepdims=True))
    cache_weights = (cache_exp / denominator).astype(jnp.bfloat16).astype(jnp.float32)
    recent_weights = (recent_exp / denominator).astype(jnp.bfloat16).astype(jnp.float32)
    summed = jnp.einsum('rkgc,rckd->rkgd', cache_weights, cache_v) + jnp.einsum('rkgs,rskd->rkgd', recent_weights, recent_v)
    return summed.reshape(row_count, kv_heads * group_size * HD).astype(jnp.bfloat16)

def reference(hidden, cache_len, layer_index, pre_gain, post_gain, w_query, w_key, w_value, w_out, cache_keys, cache_values, wide_factors, narrow_factors, wide_momentum, narrow_momentum, wide_gradient, narrow_gradient):
    layer_pick = layer_index[0]

    def select(array):
        return lax.dynamic_index_in_dim(array, layer_pick, 0, keepdims=False)
    wide_new = (select(wide_factors) - LEARN_RATE * (MOMENTUM_DECAY * select(wide_momentum) + select(wide_gradient))).astype(jnp.bfloat16)
    narrow_new = (select(narrow_factors) - LEARN_RATE * (MOMENTUM_DECAY * select(narrow_momentum) + select(narrow_gradient))).astype(jnp.bfloat16)
    merged_query = (w_query.astype(jnp.float32) + jnp.dot(wide_new[0].T, narrow_new[0], preferred_element_type=jnp.float32)).astype(jnp.bfloat16)
    merged_out = (w_out.astype(jnp.float32) + jnp.dot(narrow_new[1].T, wide_new[1], preferred_element_type=jnp.float32)).astype(jnp.bfloat16)
    row_count = hidden.shape[0]
    block_count = row_count // ROWS
    residual = hidden
    fresh_keys = jnp.zeros((row_count, STEPS, w_key.shape[1]), jnp.bfloat16)
    fresh_values = jnp.zeros((row_count, STEPS, w_value.shape[1]), jnp.bfloat16)
    for turn_index in range(STEPS):
        mean_square = lax.optimization_barrier(jnp.mean(jnp.square(residual.astype(jnp.float32)), axis=1, keepdims=True))
        normed = (residual.astype(jnp.float32) * lax.rsqrt(mean_square + EPSILON) * pre_gain).astype(jnp.bfloat16)
        position = (cache_len + turn_index).astype(jnp.float32)
        queries = rotate(jnp.dot(normed, merged_query, preferred_element_type=jnp.float32), position).astype(jnp.bfloat16)
        fresh_key = rotate(jnp.dot(normed, w_key, preferred_element_type=jnp.float32), position).astype(jnp.bfloat16)
        fresh_value = jnp.dot(normed, w_value, preferred_element_type=jnp.float32).astype(jnp.bfloat16)
        fresh_keys = fresh_keys.at[:, turn_index, :].set(fresh_key)
        fresh_values = fresh_values.at[:, turn_index, :].set(fresh_value)

        def one_block(inputs):
            return attend(inputs[0], inputs[1], inputs[2], inputs[3], inputs[4], inputs[5], turn_index)
        blocked = tuple((array.reshape((block_count, ROWS) + array.shape[1:]) for array in (queries, cache_keys, cache_values, fresh_keys, fresh_values, cache_len)))
        attended = lax.map(one_block, blocked).reshape(row_count, queries.shape[1])
        branch = jnp.dot(attended, merged_out, preferred_element_type=jnp.float32)
        row_scale = lax.rsqrt(lax.optimization_barrier(jnp.mean(branch * branch, axis=1, keepdims=True)) + EPSILON)
        residual = (residual.astype(jnp.float32) + branch * row_scale * post_gain).astype(jnp.bfloat16)
    return residual
```

```python
import functools

import jax
import jax.numpy as jnp
from jax import lax
from jax.experimental import pallas as pl
from jax.experimental.pallas import tpu as pltpu
from jax.sharding import PartitionSpec as P

D = 4608
HQ = 32
HD = 128
R = 64
ROWS = 96
CACHE = 96
STEPS = 4
QW = 256
NX = 4
NZ = 4
BR = ROWS // NX
SW = D // (NX * NZ)
HALF = SW // 2

LEARN_RATE = 0.25
MOMENTUM_DECAY = 0.9
EPSILON = 1e-06
SOFT_CAP = 50.0
ROPE_BASE = 10000.0
SCORE_SCALE = (D / HQ) ** (-0.5)

F32 = jnp.float32
BF16 = jnp.bfloat16


def send_x(value, shift):
    pairs = [(z * NX + x, z * NX + (x + shift) % NX) for z in range(NZ) for x in range(NX)]
    return lax.ppermute(value, "tensor", pairs)


def send_z(value, shift):
    pairs = [(z * NX + x, ((z + shift) % NZ) * NX + x) for z in range(NZ) for x in range(NX)]
    return lax.ppermute(value, "tensor", pairs)


def send_y(value, shift):
    pairs = [
        (w * 8 + y * 2 + c, w * 8 + ((y + shift) % 4) * 2 + c)
        for w in range(2)
        for y in range(4)
        for c in range(2)
    ]
    return lax.ppermute(value, "group", pairs)


def send_w(value):
    return lax.ppermute(value, "group", [(g, (g + 8) % 16) for g in range(16)])


def send_core(value):
    return lax.ppermute(value, "group", [(g, g ^ 1) for g in range(16)])


def gather_x(value):
    return [value] + [send_x(value, -j) for j in range(1, NX)]


def gather_z(value):
    return [value] + [send_z(value, -j) for j in range(1, NZ)]


def from_ahead(blocks, place):
    return lax.dynamic_slice_in_dim(jnp.stack(blocks + blocks), (4 - place) % 4, 4, 0)


def from_behind(blocks, place):
    turned = [blocks[0], blocks[3], blocks[2], blocks[1]]
    return from_ahead(turned, place)


def swap_x(pieces, place):
    parts = [lax.dynamic_index_in_dim(pieces, (place + j) % NX, 0, keepdims=False) for j in range(NX)]
    return from_behind([parts[0]] + [send_x(parts[j], j) for j in range(1, NX)], place)


def norm_kernel(p0, p1, p2, p3, res_ref, post_ref, pre_ref, res_out, normed_out):
    branch = (p0[...].astype(F32) + p1[...].astype(F32)) + (p2[...].astype(F32) + p3[...].astype(F32))
    scale = lax.rsqrt(jnp.mean(branch * branch, axis=1, keepdims=True) + EPSILON)
    residual = (res_ref[...].astype(F32) + branch * scale * post_ref[...]).astype(BF16)
    res_out[...] = residual
    residual = residual.astype(F32)
    scale = lax.rsqrt(jnp.mean(residual * residual, axis=1, keepdims=True) + EPSILON)
    normed_out[...] = (residual * scale * pre_ref[...]).astype(BF16)


def norm_update(partials, residual, post_gain, pre_gain):
    shape = jax.ShapeDtypeStruct((BR, D), BF16)
    return pl.pallas_call(
        norm_kernel,
        out_shape=(shape, shape),
        compiler_params=pltpu.CompilerParams(vmem_limit_bytes=24 * 2**20),
        cost_estimate=pl.CostEstimate(flops=BR * D * 10, bytes_accessed=BR * D * 14, transcendentals=0),
    )(*partials, residual, post_gain, pre_gain)


def merge_kernel(place_ref, o0, o1, o2, o3, t0, t1, t2, t3, nq_ref, na_ref, wq_ref, wo_ref, mq_ref, mo_ref, wide):
    x, z, c = place_ref[0], place_ref[1], place_ref[2]
    for core, pieces in ((c, (o0, o1, o2, o3)), (1 - c, (t0, t1, t2, t3))):
        for jx in range(NX):
            for jz in range(NZ):
                t = lax.rem(z + jz, NZ) * NX + lax.rem(x + jx, NX)
                wide[t * 2 + core] = pieces[jx][jz]
    zeros = jnp.zeros((R, QW), F32)
    nq = nq_ref[...].astype(F32)
    na = na_ref[...].astype(F32)
    b_q = jnp.concatenate([jnp.concatenate([nq[:R], nq[R:]], axis=1), zeros], axis=0).astype(BF16)
    a_o = jnp.concatenate([zeros, jnp.concatenate([na[:R], na[R:]], axis=1)], axis=0)
    a_o = a_o.T.astype(BF16)
    step = 576
    for i in range(D // step):
        block = wide[i * 4 : i * 4 + 4].reshape(step, 2 * R)
        rows = slice(i * step, (i + 1) * step)
        mq_ref[rows, :] = (
            wq_ref[rows, :].astype(F32) + jnp.dot(block, b_q, preferred_element_type=F32)
        ).astype(BF16)
    whole = wide[...].reshape(D, 2 * R)
    step = 512
    for i in range(D // step):
        cols = slice(i * step, (i + 1) * step)
        delta = lax.dot_general(
            a_o, whole[cols, :], (((1,), (1,)), ((), ())), preferred_element_type=F32
        )
        mo_ref[:, cols] = (wo_ref[:, cols].astype(F32) + delta).astype(BF16)


def merge(place, own, other, nq, na, w_query, w_out):
    smem = pl.BlockSpec(memory_space=pltpu.SMEM)
    vmem = pl.BlockSpec(memory_space=pltpu.VMEM)
    return pl.pallas_call(
        merge_kernel,
        out_shape=(jax.ShapeDtypeStruct((D, QW), BF16), jax.ShapeDtypeStruct((QW, D), BF16)),
        in_specs=[smem] + [vmem] * 12,
        out_specs=(vmem, vmem),
        scratch_shapes=[pltpu.VMEM((2 * NX * NZ, HALF, 2 * R), BF16)],
        compiler_params=pltpu.CompilerParams(vmem_limit_bytes=32 * 2**20),
        cost_estimate=pl.CostEstimate(flops=4 * D * QW * 128, bytes_accessed=12 * 2**20, transcendentals=0),
    )(place, *own, *other, nq, na, w_query, w_out)


def soft(score):
    return jnp.exp(SOFT_CAP * jnp.tanh(score * (SCORE_SCALE / SOFT_CAP)))


def step_kernel(turn, *refs):
    place_ref, n0, n1, n2, n3, len_ref, cos_ref, sin_ref = refs[:8]
    old = refs[8 : 8 + 2 * turn]
    wq_hbm, wkv_hbm, wo_hbm, k_hbm, v_hbm = refs[8 + 2 * turn : 13 + 2 * turn]
    outs = refs[13 + 2 * turn : 19 + 2 * turn]
    wq, wkv, wo, kc, vc, att, sems = refs[19 + 2 * turn :]
    x = place_ref[0]
    chunks = 4
    depth = D // chunks
    copies = []
    for i in range(chunks):
        rows = pl.ds(i * depth, depth)
        copies.append(pltpu.make_async_copy(wq_hbm.at[rows], wq.at[rows], sems.at[2 * i]))
        copies.append(pltpu.make_async_copy(wkv_hbm.at[rows], wkv.at[rows], sems.at[2 * i + 1]))
    copies.append(pltpu.make_async_copy(k_hbm, kc, sems.at[8]))
    copies.append(pltpu.make_async_copy(v_hbm, vc, sems.at[9]))
    copies.append(pltpu.make_async_copy(wo_hbm, wo, sems.at[10]))
    for copy in copies:
        copy.start()
    q = jnp.zeros((ROWS, QW), F32)
    kv = jnp.zeros((ROWS, 2 * HD), F32)
    for i in range(chunks):
        cols = slice(i * depth, (i + 1) * depth)
        normed = jnp.concatenate([n[:, cols].astype(F32) for n in (n0, n1, n2, n3)], axis=0).astype(BF16)
        copies[2 * i].wait()
        q = q + jnp.dot(normed, wq[cols, :], preferred_element_type=F32)
        copies[2 * i + 1].wait()
        kv = kv + jnp.dot(normed, wkv[cols, :], preferred_element_type=F32)
    cosine = cos_ref[turn]
    sine = sin_ref[turn]

    def rope(matrix):
        return (matrix * cosine + pltpu.roll(matrix, HD // 2, 1) * sine).astype(BF16)

    q0 = rope(q[:, :HD])
    q1 = rope(q[:, HD:])
    fresh_k = rope(kv[:, :HD])
    fresh_v = kv[:, HD:].astype(BF16)
    outs[4][...] = fresh_k
    outs[5][...] = fresh_v
    q0, q1 = q0.astype(F32), q1.astype(F32)
    keys = [old[2 * s][...].astype(F32) for s in range(turn)] + [fresh_k.astype(F32)]
    values = [old[2 * s + 1][...].astype(F32) for s in range(turn)] + [fresh_v.astype(F32)]
    new0 = [soft(jnp.sum(q0 * k, axis=1, keepdims=True)) for k in keys]
    new1 = [soft(jnp.sum(q1 * k, axis=1, keepdims=True)) for k in keys]
    new_sum0 = sum(new0[1:], new0[0])
    new_sum1 = sum(new1[1:], new1[0])
    copies[8].wait()
    column = lax.broadcasted_iota(jnp.int32, (16, 8 * CACHE), 1)
    row = lax.rem(lax.broadcasted_iota(jnp.int32, (16, 1), 0), 8)
    weights = []
    inverse = []
    for i in range(ROWS // 8):
        here = slice(8 * i, 8 * i + 8)
        base = lax.rem(x + i // 3, NX) * BR + (i % 3) * 8
        queries = jnp.concatenate([q0[here], q1[here]], axis=0).astype(BF16)
        block = kc[pl.ds(base, 8)].reshape(8 * CACHE, HD)
        score = lax.dot_general(
            queries, block, (((1,), (1,)), ((), ())), preferred_element_type=F32
        )
        length = len_ref[here]
        length = jnp.concatenate([length, length], axis=0)
        low = row * CACHE
        mask = (column >= low) & (column < low + length)
        value = jnp.where(mask, soft(score), 0.0)
        total = jnp.sum(value, axis=1, keepdims=True)
        total = total + jnp.concatenate([new_sum0[here], new_sum1[here]], axis=0)
        inv = 1.0 / total
        inverse.append(inv)
        weights.append((value * inv).astype(BF16))
    inv0 = jnp.concatenate([inv[:8] for inv in inverse], axis=0)
    inv1 = jnp.concatenate([inv[8:] for inv in inverse], axis=0)

    def recent(new, inv):
        total = None
        for w, v in zip(new, values):
            term = (w * inv).astype(BF16).astype(F32) * v
            total = term if total is None else total + term
        return total

    add0 = recent(new0, inv0)
    add1 = recent(new1, inv1)
    copies[9].wait()
    for i in range(ROWS // 8):
        here = slice(8 * i, 8 * i + 8)
        base = lax.rem(x + i // 3, NX) * BR + (i % 3) * 8
        block = vc[pl.ds(base, 8)].reshape(8 * CACHE, HD)
        summed = jnp.dot(weights[i], block, preferred_element_type=F32)
        att[here, :HD] = summed[:8] + add0[here]
        att[here, HD:] = summed[8:] + add1[here]
    attended = att[...].astype(BF16)
    copies[10].wait()
    width = 512
    for i in range(D // width):
        cols = slice(i * width, (i + 1) * width)
        part = jnp.dot(attended, wo[:, cols], preferred_element_type=F32)
        for j in range(NX):
            outs[j][:, cols] = part[j * BR : (j + 1) * BR].astype(BF16)


def step(turn, place, normed, lengths, cosine, sine, old, w_query, w_kv, w_out, keys, values):
    smem = pl.BlockSpec(memory_space=pltpu.SMEM)
    vmem = pl.BlockSpec(memory_space=pltpu.VMEM)
    hbm = pl.BlockSpec(memory_space=pl.ANY)
    block = jax.ShapeDtypeStruct((BR, D), BF16)
    fresh = jax.ShapeDtypeStruct((ROWS, HD), BF16)
    return pl.pallas_call(
        functools.partial(step_kernel, turn),
        out_shape=(block,) * 4 + (fresh,) * 2,
        in_specs=[smem] + [vmem] * (7 + 2 * turn) + [hbm] * 5,
        out_specs=(vmem,) * 6,
        scratch_shapes=[
            pltpu.VMEM((D, QW), BF16),
            pltpu.VMEM((D, 2 * HD), BF16),
            pltpu.VMEM((QW, D), BF16),
            pltpu.VMEM((ROWS, CACHE, HD), BF16),
            pltpu.VMEM((ROWS, CACHE, HD), BF16),
            pltpu.VMEM((ROWS, QW), F32),
            pltpu.SemaphoreType.DMA((11,)),
        ],
        compiler_params=pltpu.CompilerParams(vmem_limit_bytes=40 * 2**20),
        cost_estimate=pl.CostEstimate(flops=2 * ROWS * D * 768, bytes_accessed=13 * 2**20, transcendentals=0),
    )(place, *normed, lengths, cosine, sine, *old, w_query, w_kv, w_out, keys, values)


def body(
    hidden,
    cache_len,
    layer_index,
    pre_gain,
    post_gain,
    w_query,
    w_key,
    w_value,
    w_out,
    cache_keys,
    cache_values,
    wide_factors,
    narrow_factors,
    wide_momentum,
    narrow_momentum,
    wide_gradient,
    narrow_gradient,
):
    tensor = lax.axis_index("tensor")
    group = lax.axis_index("group")
    x = tensor % NX
    z = tensor // NX
    core = group % 2
    place = jnp.stack([x, z, core]).astype(jnp.int32)

    layers_here = wide_factors.shape[0]
    owner = layer_index[0] // layers_here
    slot = layer_index[0] % layers_here

    def updated(factors, momentum, gradient):
        def pick(a):
            return lax.dynamic_index_in_dim(a, slot, 0, keepdims=False)

        new = (pick(factors) - LEARN_RATE * (MOMENTUM_DECAY * pick(momentum) + pick(gradient))).astype(BF16)
        return jnp.where(owner == group, new, jnp.zeros_like(new))

    wide = updated(wide_factors, wide_momentum, wide_gradient)
    narrow = updated(narrow_factors, narrow_momentum, narrow_gradient)
    wide = wide.transpose(2, 0, 1).reshape(2, HALF, 2 * R)
    narrow = narrow.reshape(2, R, 2, HD).transpose(0, 2, 1, 3).reshape(2, 2 * R, HD)
    load = jnp.concatenate([wide, narrow], axis=1)
    mine = lax.dynamic_index_in_dim(load, core, 0, keepdims=False)
    theirs = lax.dynamic_index_in_dim(load, 1 - core, 0, keepdims=False)
    mine = mine + send_core(theirs)
    mine = mine + send_y(mine, 1) + send_y(mine, 2) + send_y(mine, 3)
    mine = mine + send_w(mine)
    small = mine[HALF:]
    column = jnp.stack(gather_z(mine[:HALF]))
    own = gather_x(column)
    other = [send_core(v) for v in own]
    small_other = send_core(small)
    nq = jnp.where(core == 0, small, small_other)
    na = jnp.where(core == 0, small_other, small)

    pieces = swap_x(hidden.reshape(NX, BR, SW), x)
    pieces = pieces.transpose(1, 0, 2).reshape(BR, NX * SW)
    residual = from_ahead(gather_z(pieces), z).transpose(1, 0, 2).reshape(BR, D)
    res32 = residual.astype(F32)
    mean_square = jnp.mean(jnp.square(res32), axis=1, keepdims=True)
    normed = (res32 * lax.rsqrt(mean_square + EPSILON) * pre_gain).astype(BF16)

    lengths = jnp.concatenate([cache_len, cache_len])
    lengths = lax.dynamic_slice_in_dim(lengths, x * BR, ROWS, 0)
    frequency = ROPE_BASE ** (-jnp.arange(HD // 2, dtype=F32) * 2.0 / HD)
    position = (lengths[None, :] + jnp.arange(STEPS)[:, None]).astype(F32)
    angles = position[:, :, None] * frequency
    cosine = jnp.cos(angles)
    sine = jnp.sin(angles)
    cosine = jnp.concatenate([cosine, cosine], axis=-1)
    sine = jnp.concatenate([-sine, sine], axis=-1)
    lengths = lengths[:, None]
    w_kv = jnp.concatenate([w_key, w_value], axis=1)
    pre = pre_gain[None, :]
    post = post_gain[None, :]

    merged_query, merged_out = merge(place, own, other, nq, na, w_query, w_out)

    old = []
    for turn in range(STEPS):
        blocks = gather_x(normed)
        *partial, fresh_k, fresh_v = step(
            turn, place, blocks, lengths, cosine, sine, old, merged_query, w_kv, merged_out, cache_keys, cache_values
        )
        old = old + [fresh_k, fresh_v]
        arrived = [partial[0]] + [send_x(partial[j], j) for j in range(1, NX)]
        summed = sum([a.astype(F32) for a in arrived[1:]], arrived[0].astype(F32)).astype(BF16)
        residual, normed = norm_update(gather_z(summed), residual, post, pre)

    mine = lax.dynamic_slice_in_dim(residual, z * NX * SW, NX * SW, 1)
    mine = mine.reshape(BR, NX, SW).transpose(1, 0, 2)
    return swap_x(mine, x).reshape(ROWS, SW)


def solution(mesh):
    rows = P("group", "tensor")
    columns = P(None, "tensor")
    cache = P("group", None, "tensor")
    state = P("group", None, None, "tensor")
    in_specs = (
        rows,
        P("group"),
        P(),
        P(),
        P(),
        columns,
        columns,
        columns,
        P("tensor", None),
        cache,
        cache,
    ) + (state,) * 6
    return jax.shard_map(body, mesh=mesh, in_specs=in_specs, out_specs=rows, check_vma=False)
```

```python
import functools

import jax
import jax.numpy as jnp
from jax import lax
from jax.experimental import pallas as pl
from jax.experimental.pallas import tpu as pltpu
from jax.sharding import PartitionSpec as P

D = 4608
HQ = 32
HD = 128
R = 64
ROWS = 96
CACHE = 96
STEPS = 4
QW = 256
NX = 4
NZ = 4
SW = D // (NX * NZ)
BW = D // NX
HALF = SW // 2
STREAMS = 2
SR = ROWS // STREAMS

LEARN_RATE = 0.25
MOMENTUM_DECAY = 0.9
EPSILON = 1e-06
SOFT_CAP = 50.0
ROPE_BASE = 10000.0
SCORE_SCALE = (D / HQ) ** (-0.5)

F32 = jnp.float32
BF16 = jnp.bfloat16
MIB = 2**20


def send_x(value, shift):
    pairs = [(z * NX + x, z * NX + (x + shift) % NX) for z in range(NZ) for x in range(NX)]
    return lax.ppermute(value, "tensor", pairs)


def send_z(value, shift):
    pairs = [(z * NX + x, ((z + shift) % NZ) * NX + x) for z in range(NZ) for x in range(NX)]
    return lax.ppermute(value, "tensor", pairs)


def send_y(value, shift):
    pairs = [
        (w * 8 + y * 2 + c, w * 8 + ((y + shift) % 4) * 2 + c)
        for w in range(2)
        for y in range(4)
        for c in range(2)
    ]
    return lax.ppermute(value, "group", pairs)


def send_w(value):
    return lax.ppermute(value, "group", [(g, (g + 8) % 16) for g in range(16)])


def send_core(value):
    return lax.ppermute(value, "group", [(g, g ^ 1) for g in range(16)])


def gather_x(value):
    return [value] + [send_x(value, -j) for j in range(1, NX)]


def gather_z(value):
    return [value] + [send_z(value, -j) for j in range(1, NZ)]


def after(value, earlier):
    return lax.optimization_barrier((value, earlier))[0]


def smem():
    return pl.BlockSpec(memory_space=pltpu.SMEM)


def vmem():
    return pl.BlockSpec(memory_space=pltpu.VMEM)


def by_x(array, x):
    return jnp.concatenate([array[:, (z * NX + x) * SW : (z * NX + x + 1) * SW] for z in range(NZ)], axis=1)


def arrange_kernel(place_ref, wk_ref, wv_ref, post_ref, pre_ref, out_ref, post_out, pre_out):
    x = place_ref[0]
    for j in range(NX):
        for z in range(NZ):
            t = z * NX + lax.rem(x + j, NX)
            out_ref[j * NZ + z, :, :HD] = wk_ref[t]
            out_ref[j * NZ + z, :, HD:] = wv_ref[t]
    for there in range(NX):
        j = lax.rem(there - x + NX, NX)
        post_out[j] = by_x(post_ref[...], there)
        pre_out[j] = by_x(pre_ref[...], there)


def arrange(place, w_key, w_value, post_gain, pre_gain):
    gain = jax.ShapeDtypeStruct((NX, 1, BW), F32)
    out, post, pre = pl.pallas_call(
        arrange_kernel,
        out_shape=(jax.ShapeDtypeStruct((NX * NZ, SW, 2 * HD), BF16), gain, gain),
        in_specs=[smem()] + [vmem()] * 4,
        out_specs=(vmem(),) * 3,
        compiler_params=pltpu.CompilerParams(vmem_limit_bytes=16 * MIB),
        cost_estimate=pl.CostEstimate(flops=0, bytes_accessed=5 * MIB, transcendentals=0),
    )(place, w_key.reshape(NX * NZ, SW, HD), w_value.reshape(NX * NZ, SW, HD), post_gain[None], pre_gain[None])
    return out.reshape(NX, BW, 2 * HD), post.reshape(NX, BW), pre.reshape(NX, BW)


def split_kernel(place_ref, w_ref, home_out, o1, o2, o3, rolled):
    x, c = place_ref[0], place_ref[2]
    for there in range(NX):
        piece = by_x(w_ref[...], there)
        j = lax.rem(x - there + NX, NX)
        rolled[j, 0] = piece[: QW // 2]
        rolled[j, 1] = piece[QW // 2 :]
    home_out[...] = rolled[0].reshape(QW, BW)
    for j, out in enumerate((o1, o2, o3)):
        out[...] = rolled[j + 1, c]


def split(place, w_out):
    half = jax.ShapeDtypeStruct((QW // 2, BW), BF16)
    return pl.pallas_call(
        split_kernel,
        out_shape=(jax.ShapeDtypeStruct((QW, BW), BF16), half, half, half),
        in_specs=[smem(), vmem()],
        out_specs=(vmem(),) * NX,
        scratch_shapes=[pltpu.VMEM((NX, 2, QW // 2, BW), BF16)],
        compiler_params=pltpu.CompilerParams(vmem_limit_bytes=20 * MIB),
        cost_estimate=pl.CostEstimate(flops=0, bytes_accessed=5 * MIB, transcendentals=0),
    )(place, w_out)


def join_kernel(place_ref, p0, p1, p2, p3, out_ref, rolled):
    z = place_ref[1]
    for j, piece in enumerate((p0, p1, p2, p3)):
        rolled[lax.rem(z + j, NZ)] = piece[...]
    out_ref[...] = jnp.concatenate([rolled[i] for i in range(NZ)], axis=1)


def join(place, pieces):
    return pl.pallas_call(
        join_kernel,
        out_shape=jax.ShapeDtypeStruct((ROWS, BW), BF16),
        in_specs=[smem()] + [vmem()] * NZ,
        out_specs=vmem(),
        scratch_shapes=[pltpu.VMEM((NZ, ROWS, SW), BF16)],
        compiler_params=pltpu.CompilerParams(vmem_limit_bytes=4 * MIB),
        cost_estimate=pl.CostEstimate(flops=0, bytes_accessed=MIB // 2, transcendentals=0),
    )(place, *pieces)


def factor_kernel(place_ref, *refs):
    wide_hbm, narrow_hbm = refs[0:3], refs[3:6]
    mine_out, theirs_out = refs[6:8]
    wide_in, narrow_in, wide, sems = refs[8:]
    c, owned, slot = place_ref[2], place_ref[3], place_ref[4]
    copies = []
    for i in range(3):
        copies.append(pltpu.make_async_copy(wide_hbm[i].at[slot], wide_in.at[i], sems.at[i]))
        copies.append(pltpu.make_async_copy(narrow_hbm[i].at[slot], narrow_in.at[i], sems.at[3 + i]))
    for copy in copies:
        copy.start()
    for copy in copies:
        copy.wait()

    def update(old, momentum, gradient):
        new = old - LEARN_RATE * (MOMENTUM_DECAY * momentum + gradient)
        return jnp.where(owned == 1, new, 0.0)

    new = update(wide_in[0], wide_in[1], wide_in[2]).reshape(2 * R, SW)
    new = jnp.concatenate([new, jnp.zeros((2 * R, 96), F32)], axis=1)
    wide[...] = new.T
    for out, member in ((mine_out, c), (theirs_out, 1 - c)):
        out[:HALF, :] = wide[pl.ds(pl.multiple_of(member * HALF, 8), HALF), :].astype(BF16)
        new = update(narrow_in[0, member], narrow_in[1, member], narrow_in[2, member]).astype(BF16)
        out[HALF : HALF + R, :] = new[:, :HD]
        out[HALF + R :, :] = new[:, HD:]


def new_factors(place, wide, narrow):
    out = jax.ShapeDtypeStruct((HALF + 2 * R, 2 * R), BF16)
    return pl.pallas_call(
        factor_kernel,
        out_shape=(out, out),
        in_specs=[smem()] + [pl.BlockSpec(memory_space=pl.ANY)] * 6,
        out_specs=(vmem(), vmem()),
        scratch_shapes=[
            pltpu.VMEM((3, 2, R, SW), F32),
            pltpu.VMEM((3, 2, R, QW), F32),
            pltpu.VMEM((SW + 96, 2 * R), F32),
            pltpu.SemaphoreType.DMA((6,)),
        ],
        compiler_params=pltpu.CompilerParams(vmem_limit_bytes=4 * MIB),
        cost_estimate=pl.CostEstimate(flops=0, bytes_accessed=MIB, transcendentals=0),
    )(place, *wide, *narrow)


def both_halves(nq):
    nq = nq.astype(F32)
    return jnp.concatenate([nq[:R], nq[R:]], axis=1)


def merge_query_kernel(place_ref, own_ref, other_ref, wq_ref, out_ref, b_q):
    x, z, c = place_ref[0], place_ref[1], place_ref[2]
    zeros = jnp.zeros((R, QW), F32)

    @pl.when(c == 0)
    def _():
        b_q[...] = jnp.concatenate([both_halves(own_ref[0, NZ * HALF :]), zeros], axis=0).astype(BF16)

    @pl.when(c == 1)
    def _():
        b_q[...] = jnp.concatenate([both_halves(other_ref[0, NZ * HALF :]), zeros], axis=0).astype(BF16)

    factor = b_q[...]
    for core, pieces in ((c, own_ref), (1 - c, other_ref)):
        for jx in range(NX):
            for jz in range(NZ):
                there = lax.rem(z + jz, NZ)
                source = (there * NX + lax.rem(x + jx, NX)) * 2 + core
                target = (jx * NZ + there) * 2 + core
                piece = pieces[jx, jz * HALF : (jz + 1) * HALF]
                delta = jnp.dot(piece, factor, preferred_element_type=F32)
                out_ref[target] = (wq_ref[source].astype(F32) + delta).astype(BF16)


def merge_query(place, own, other, w_query):
    out = pl.pallas_call(
        merge_query_kernel,
        out_shape=jax.ShapeDtypeStruct((2 * NX * NZ, HALF, QW), BF16),
        in_specs=[smem()] + [vmem()] * 3,
        out_specs=vmem(),
        scratch_shapes=[pltpu.VMEM((2 * R, QW), BF16)],
        compiler_params=pltpu.CompilerParams(vmem_limit_bytes=20 * MIB),
        cost_estimate=pl.CostEstimate(flops=2 * D * QW * 128, bytes_accessed=6 * MIB, transcendentals=0),
    )(place, own, other, w_query.reshape(2 * NX * NZ, HALF, QW))
    return out.reshape(NX, BW, QW)


def merge_out_kernel(place_ref, own_ref, other_ref, home_ref, *refs):
    z, c = place_ref[1], place_ref[2]
    mine, theirs = refs[0:3], refs[3:6]
    out_ref, wide, small, delta = refs[6:]
    for core, pieces in ((c, own_ref), (1 - c, other_ref)):
        for jz in range(NZ):
            wide[lax.rem(z + jz, NZ) * 2 + core] = pieces[0, jz * HALF : (jz + 1) * HALF]
        small[core] = pieces[:, NZ * HALF :]
    b_o = wide[...].reshape(BW, 2 * R)
    zeros = jnp.zeros((R, QW), F32)
    for j in range(NX):
        a_o = jnp.concatenate([zeros, both_halves(small[1, j])], axis=0).T.astype(BF16)
        change = lax.dot_general(a_o, b_o, (((1,), (1,)), ((), ())), preferred_element_type=F32)
        change = change.reshape(2, QW // 2, BW)
        if j == 0:
            out_ref[0] = (home_ref[...].astype(F32).reshape(2, QW // 2, BW) + change).astype(BF16)
        else:
            delta[...] = change
            out_ref[j, c] = (mine[j - 1][...].astype(F32) + delta[c]).astype(BF16)
            out_ref[j, 1 - c] = (theirs[j - 1][...].astype(F32) + delta[1 - c]).astype(BF16)


def merge_out(place, own, other, home, mine, theirs):
    out = pl.pallas_call(
        merge_out_kernel,
        out_shape=jax.ShapeDtypeStruct((NX, 2, QW // 2, BW), BF16),
        in_specs=[smem()] + [vmem()] * 9,
        out_specs=vmem(),
        scratch_shapes=[
            pltpu.VMEM((2 * NZ, HALF, 2 * R), BF16),
            pltpu.VMEM((2, NX, 2 * R, 2 * R), BF16),
            pltpu.VMEM((2, QW // 2, BW), F32),
        ],
        compiler_params=pltpu.CompilerParams(vmem_limit_bytes=24 * MIB),
        cost_estimate=pl.CostEstimate(flops=2 * D * QW * 128, bytes_accessed=6 * MIB, transcendentals=0),
    )(place, own, other, home, *mine, *theirs)
    return out.reshape(NX * QW, BW)


def soft(score):
    return jnp.exp(SOFT_CAP * jnp.tanh(score * (SCORE_SCALE / SOFT_CAP)))


def step_kernel(turn, stream, *refs):
    refs = list(refs)

    def take(count):
        taken = refs[:count]
        del refs[:count]
        return taken

    start = stream * SR
    mine = slice(start, start + SR)
    if turn == 0:
        held = [ref[mine, :].astype(F32) for ref in take(NX)]
    else:
        branch = [ref[...].astype(F32) for ref in take(NX)]
        (res_ref,) = take(1)
    post_ref, pre_ref, len_ref, cos_ref, sin_ref = take(5)
    old = take(2 * turn)
    wq, wkv, kc, vc = take(4)
    res_out, att_out, fk_out, fv_out = take(4)
    if turn > 0:
        square = sum(jnp.sum(b * b, axis=1, keepdims=True) for b in branch)
        scale = lax.rsqrt(square * (1.0 / D) + EPSILON)
        held = [
            (res_ref[j].astype(F32) + branch[j] * scale * post_ref[j : j + 1, :]).astype(BF16).astype(F32)
            for j in range(NX)
        ]
    square = sum(jnp.sum(r * r, axis=1, keepdims=True) for r in held)
    scale = lax.rsqrt(square * (1.0 / D) + EPSILON)
    q = jnp.zeros((SR, QW), F32)
    kv = jnp.zeros((SR, 2 * HD), F32)
    for j in range(NX):
        res_out[j] = held[j].astype(BF16)
        normed = (held[j] * scale * pre_ref[j : j + 1, :]).astype(BF16)
        q = q + jnp.dot(normed, wq[j], preferred_element_type=F32)
        kv = kv + jnp.dot(normed, wkv[j], preferred_element_type=F32)
    cosine = cos_ref[turn, mine, :]
    sine = sin_ref[turn, mine, :]

    def rope(matrix):
        return (matrix * cosine + pltpu.roll(matrix, HD // 2, 1) * sine).astype(BF16)

    q0 = rope(q[:, :HD]).astype(F32)
    q1 = rope(q[:, HD:]).astype(F32)
    fresh_k = rope(kv[:, :HD])
    fresh_v = kv[:, HD:].astype(BF16)
    fk_out[...] = fresh_k
    fv_out[...] = fresh_v
    keys = [old[2 * s][...].astype(F32) for s in range(turn)] + [fresh_k.astype(F32)]
    values = [old[2 * s + 1][...].astype(F32) for s in range(turn)] + [fresh_v.astype(F32)]
    new0 = [soft(jnp.sum(q0 * k, axis=1, keepdims=True)) for k in keys]
    new1 = [soft(jnp.sum(q1 * k, axis=1, keepdims=True)) for k in keys]
    new_sum0 = sum(new0[1:], new0[0])
    new_sum1 = sum(new1[1:], new1[0])
    column = lax.broadcasted_iota(jnp.int32, (16, 8 * CACHE), 1)
    low = lax.rem(lax.broadcasted_iota(jnp.int32, (16, 1), 0), 8) * CACHE
    weights = []
    inverse = []
    for i in range(SR // 8):
        here = slice(8 * i, 8 * i + 8)
        there = slice(start + 8 * i, start + 8 * i + 8)
        queries = jnp.concatenate([q0[here], q1[here]], axis=0).astype(BF16)
        block = kc[there].reshape(8 * CACHE, HD)
        score = lax.dot_general(queries, block, (((1,), (1,)), ((), ())), preferred_element_type=F32)
        length = len_ref[there]
        length = jnp.concatenate([length, length], axis=0)
        mask = (column >= low) & (column < low + length)
        value = jnp.where(mask, soft(score), 0.0)
        total = jnp.sum(value, axis=1, keepdims=True)
        total = total + jnp.concatenate([new_sum0[here], new_sum1[here]], axis=0)
        inv = 1.0 / total
        inverse.append(inv)
        weights.append((value * inv).astype(BF16))
    inv0 = jnp.concatenate([inv[:8] for inv in inverse], axis=0)
    inv1 = jnp.concatenate([inv[8:] for inv in inverse], axis=0)

    def recent(new, inv):
        total = None
        for w, v in zip(new, values):
            term = (w * inv).astype(BF16).astype(F32) * v
            total = term if total is None else total + term
        return total

    add0 = recent(new0, inv0)
    add1 = recent(new1, inv1)
    got0 = []
    got1 = []
    for i in range(SR // 8):
        there = slice(start + 8 * i, start + 8 * i + 8)
        block = vc[there].reshape(8 * CACHE, HD)
        summed = jnp.dot(weights[i], block, preferred_element_type=F32)
        got0.append(summed[:8])
        got1.append(summed[8:])
    att_out[:, :HD] = (jnp.concatenate(got0, axis=0) + add0).astype(BF16)
    att_out[:, HD:] = (jnp.concatenate(got1, axis=0) + add1).astype(BF16)


def step(turn, stream, blocks, residual, post, pre, lengths, cosine, sine, old, w_query, w_kv, keys, values):
    fresh = jax.ShapeDtypeStruct((SR, HD), BF16)
    state = list(blocks) + ([] if turn == 0 else [residual])
    args = state + [post, pre, lengths, cosine, sine] + old + [w_query, w_kv, keys, values]
    return pl.pallas_call(
        functools.partial(step_kernel, turn, stream),
        out_shape=(
            jax.ShapeDtypeStruct((NX, SR, BW), BF16),
            jax.ShapeDtypeStruct((SR, QW), BF16),
            fresh,
            fresh,
        ),
        in_specs=[vmem()] * len(args),
        out_specs=(vmem(),) * 4,
        compiler_params=pltpu.CompilerParams(vmem_limit_bytes=28 * MIB),
        cost_estimate=pl.CostEstimate(flops=2 * SR * D * 512, bytes_accessed=10 * MIB, transcendentals=0),
    )(*args)


def project_kernel(a0, a1, a2, a3, w_ref, *outs):
    attended = jnp.concatenate([a0[...], a1[...], a2[...], a3[...]], axis=1)
    partial = jnp.dot(attended, w_ref[...], preferred_element_type=F32).astype(BF16)
    for s, out in enumerate(outs):
        out[...] = partial[s * SR : (s + 1) * SR]


def project(attended, w_out):
    return pl.pallas_call(
        project_kernel,
        out_shape=(jax.ShapeDtypeStruct((SR, BW), BF16),) * STREAMS,
        in_specs=[vmem()] * 5,
        out_specs=(vmem(),) * STREAMS,
        compiler_params=pltpu.CompilerParams(vmem_limit_bytes=16 * MIB),
        cost_estimate=pl.CostEstimate(flops=2 * ROWS * BW * 1024, bytes_accessed=3 * MIB, transcendentals=0),
    )(*attended, w_out)


def add_up(blocks):
    first, *rest = [b.astype(F32) for b in blocks]
    return sum(rest, first)


def body(
    hidden,
    cache_len,
    layer_index,
    pre_gain,
    post_gain,
    w_query,
    w_key,
    w_value,
    w_out,
    cache_keys,
    cache_values,
    wide_factors,
    narrow_factors,
    wide_momentum,
    narrow_momentum,
    wide_gradient,
    narrow_gradient,
):
    tensor = lax.axis_index("tensor")
    group = lax.axis_index("group")
    x = tensor % NX
    z = tensor // NX
    core = group % 2
    layers_here = wide_factors.shape[0]
    owner = layer_index[0] // layers_here
    slot = layer_index[0] % layers_here
    place = jnp.stack([x, z, core, owner == group, slot]).astype(jnp.int32)

    wide = [wide_factors, wide_momentum, wide_gradient]
    narrow = [narrow_factors, narrow_momentum, narrow_gradient]
    mine, theirs = new_factors(place, wide, narrow)
    mine = mine + send_core(theirs)

    pieces = gather_z(hidden)
    parts = split(after(place, mine), w_out)
    block = join(after(place, mine), pieces)

    mine = after(mine + send_y(mine, 1) + send_y(mine, 2) + send_y(mine, 3), (parts, block))
    out_mine = [send_x(parts[j], -j) for j in range(1, NX)]
    mine = mine + send_w(mine)
    blocks = gather_x(block)
    cache_len = after(cache_len, mine)
    w_kv, post, pre = arrange(after(place, mine), w_key, w_value, post_gain, pre_gain)
    column = jnp.concatenate(gather_z(mine[:HALF]) + [mine[HALF:]])
    column = after(column, (out_mine, w_kv, post, pre))
    own = jnp.stack(gather_x(column))
    other = send_core(own)
    out_theirs = [send_core(after(v, column)) for v in out_mine]

    frequency = ROPE_BASE ** (-jnp.arange(HD // 2, dtype=F32) * 2.0 / HD)
    position = (cache_len[None, :] + jnp.arange(STEPS)[:, None]).astype(F32)
    angles = position[:, :, None] * frequency
    cosine = jnp.cos(angles)
    sine = jnp.sin(angles)
    cosine = jnp.concatenate([cosine, cosine], axis=-1)
    sine = jnp.concatenate([-sine, sine], axis=-1)
    lengths = cache_len[:, None]

    merged_query = merge_query(place, own, other, w_query)
    merged_out = merge_out(place, own, other, parts[0], out_mine, out_theirs)

    blocks = [blocks] * STREAMS
    residual = [None] * STREAMS
    old = [[] for _ in range(STREAMS)]
    sums = [None] * STREAMS
    for turn in range(STEPS):
        attended = [None] * STREAMS
        for s in range(STREAMS):
            residual[s], attended[s], fresh_k, fresh_v = step(
                turn, s, blocks[s], residual[s], post, pre, lengths, cosine, sine, old[s],
                merged_query, w_kv, cache_keys, cache_values,
            )
            old[s] = old[s] + [fresh_k, fresh_v]
        partial = project(gather_x(jnp.concatenate(attended)), merged_out)
        for s in range(STREAMS):
            sums[s] = add_up(gather_z(partial[s]))
            if turn < STEPS - 1:
                blocks[s] = gather_x(sums[s].astype(BF16))

    branch = jnp.concatenate(sums, axis=0)
    home_residual = jnp.concatenate([r[0] for r in residual], axis=0).astype(F32)
    square = add_up(gather_x(jnp.sum(branch * branch, axis=1)))
    scale = lax.rsqrt(square * (1.0 / D) + EPSILON)[:, None]
    final = (home_residual + branch * scale * post[:1]).astype(BF16)
    return lax.dynamic_slice_in_dim(final, z * SW, SW, 1)


def solution(mesh):
    rows = P("group", "tensor")
    columns = P(None, "tensor")
    cache = P("group", None, "tensor")
    state = P("group", None, None, "tensor")
    in_specs = (
        rows,
        P("group"),
        P(),
        P(),
        P(),
        columns,
        columns,
        columns,
        P("tensor", None),
        cache,
        cache,
    ) + (state,) * 6
    return jax.shard_map(body, mesh=mesh, in_specs=in_specs, out_specs=rows, check_vma=False)
```

```python
import functools

import jax
import jax.numpy as jnp
from jax import lax
from jax.experimental import pallas as pl
from jax.experimental.pallas import tpu as pltpu
from jax.sharding import PartitionSpec as P

D = 4608
HQ = 32
HD = 128
R = 64
ROWS = 96
CACHE = 96
STEPS = 4
QW = 256
NX = 4
NZ = 4
SW = D // (NX * NZ)
BW = D // NX
HALF = SW // 2
BOUNDS = (0, 48, 96)
STREAMS = len(BOUNDS) - 1

LEARN_RATE = 0.25
MOMENTUM_DECAY = 0.9
EPSILON = 1e-06
SOFT_CAP = 50.0
ROPE_BASE = 10000.0
SCORE_SCALE = (D / HQ) ** (-0.5)

F32 = jnp.float32
BF16 = jnp.bfloat16
MIB = 2**20


def send_x(value, shift):
    pairs = [(z * NX + x, z * NX + (x + shift) % NX) for z in range(NZ) for x in range(NX)]
    return lax.ppermute(value, "tensor", pairs)


def send_z(value, shift):
    pairs = [(z * NX + x, ((z + shift) % NZ) * NX + x) for z in range(NZ) for x in range(NX)]
    return lax.ppermute(value, "tensor", pairs)


def send_y(value, shift):
    pairs = [
        (w * 8 + y * 2 + c, w * 8 + ((y + shift) % 4) * 2 + c)
        for w in range(2)
        for y in range(4)
        for c in range(2)
    ]
    return lax.ppermute(value, "group", pairs)


def send_w(value):
    return lax.ppermute(value, "group", [(g, (g + 8) % 16) for g in range(16)])


def send_core(value):
    return lax.ppermute(value, "group", [(g, g ^ 1) for g in range(16)])


def gather_x(value):
    return [value] + [send_x(value, -j) for j in range(1, NX)]


def gather_z(value):
    return [value] + [send_z(value, -j) for j in range(1, NZ)]


def after(value, earlier):
    return lax.optimization_barrier((value, earlier))[0]


def smem():
    return pl.BlockSpec(memory_space=pltpu.SMEM)


def vmem():
    return pl.BlockSpec(memory_space=pltpu.VMEM)


def by_x(array, x):
    return jnp.concatenate([array[:, (z * NX + x) * SW : (z * NX + x + 1) * SW] for z in range(NZ)], axis=1)


def arrange_kernel(place_ref, wk_ref, wv_ref, post_ref, pre_ref, out_ref, post_out, pre_out):
    x = place_ref[0]
    for j in range(NX):
        for z in range(NZ):
            t = z * NX + lax.rem(x + j, NX)
            out_ref[j * NZ + z, :, :HD] = wk_ref[t]
            out_ref[j * NZ + z, :, HD:] = wv_ref[t]
    for there in range(NX):
        j = lax.rem(there - x + NX, NX)
        post_out[j] = by_x(post_ref[...], there)
        pre_out[j] = by_x(pre_ref[...], there)


def arrange(place, w_key, w_value, post_gain, pre_gain):
    gain = jax.ShapeDtypeStruct((NX, 1, BW), F32)
    out, post, pre = pl.pallas_call(
        arrange_kernel,
        out_shape=(jax.ShapeDtypeStruct((NX * NZ, SW, 2 * HD), BF16), gain, gain),
        in_specs=[smem()] + [vmem()] * 4,
        out_specs=(vmem(),) * 3,
        compiler_params=pltpu.CompilerParams(vmem_limit_bytes=14 * MIB),
        cost_estimate=pl.CostEstimate(flops=0, bytes_accessed=5 * MIB, transcendentals=0),
    )(place, w_key.reshape(NX * NZ, SW, HD), w_value.reshape(NX * NZ, SW, HD), post_gain[None], pre_gain[None])
    return out.reshape(NX, BW, 2 * HD), post.reshape(NX, BW), pre.reshape(NX, BW)


def split_kernel(place_ref, w_ref, home_out, o1, o2, o3, rolled):
    x, c = place_ref[0], place_ref[2]
    for there in range(NX):
        piece = by_x(w_ref[...], there)
        j = lax.rem(x - there + NX, NX)
        rolled[j, 0] = piece[: QW // 2]
        rolled[j, 1] = piece[QW // 2 :]
    home_out[...] = rolled[0].reshape(QW, BW)
    for j, out in enumerate((o1, o2, o3)):
        out[...] = rolled[j + 1, c]


def split(place, w_out):
    half = jax.ShapeDtypeStruct((QW // 2, BW), BF16)
    return pl.pallas_call(
        split_kernel,
        out_shape=(jax.ShapeDtypeStruct((QW, BW), BF16), half, half, half),
        in_specs=[smem(), vmem()],
        out_specs=(vmem(),) * NX,
        scratch_shapes=[pltpu.VMEM((NX, 2, QW // 2, BW), BF16)],
        compiler_params=pltpu.CompilerParams(vmem_limit_bytes=12 * MIB),
        cost_estimate=pl.CostEstimate(flops=0, bytes_accessed=5 * MIB, transcendentals=0),
    )(place, w_out)


def join_kernel(place_ref, p0, p1, p2, p3, out_ref, rolled):
    z = place_ref[1]
    for j, piece in enumerate((p0, p1, p2, p3)):
        rolled[lax.rem(z + j, NZ)] = piece[...]
    out_ref[...] = jnp.concatenate([rolled[i] for i in range(NZ)], axis=1)


def join(place, pieces):
    return pl.pallas_call(
        join_kernel,
        out_shape=jax.ShapeDtypeStruct((ROWS, BW), BF16),
        in_specs=[smem()] + [vmem()] * NZ,
        out_specs=vmem(),
        scratch_shapes=[pltpu.VMEM((NZ, ROWS, SW), BF16)],
        compiler_params=pltpu.CompilerParams(vmem_limit_bytes=4 * MIB),
        cost_estimate=pl.CostEstimate(flops=0, bytes_accessed=MIB // 2, transcendentals=0),
    )(place, *pieces)


def factor_kernel(place_ref, *refs):
    wide_hbm, narrow_hbm = refs[0:3], refs[3:6]
    mine_out, theirs_out = refs[6:8]
    wide_in, narrow_in, wide, sems = refs[8:]
    c, owned, slot = place_ref[2], place_ref[3], place_ref[4]
    copies = []
    for i in range(3):
        copies.append(pltpu.make_async_copy(wide_hbm[i].at[slot], wide_in.at[i], sems.at[i]))
        copies.append(pltpu.make_async_copy(narrow_hbm[i].at[slot], narrow_in.at[i], sems.at[3 + i]))
    for copy in copies:
        copy.start()
    for copy in copies:
        copy.wait()

    def update(old, momentum, gradient):
        new = old - LEARN_RATE * (MOMENTUM_DECAY * momentum + gradient)
        return jnp.where(owned == 1, new, 0.0)

    new = update(wide_in[0], wide_in[1], wide_in[2]).reshape(2 * R, SW)
    new = jnp.concatenate([new, jnp.zeros((2 * R, 96), F32)], axis=1)
    wide[...] = new.T
    for out, member in ((mine_out, c), (theirs_out, 1 - c)):
        out[:HALF, :] = wide[pl.ds(pl.multiple_of(member * HALF, 8), HALF), :].astype(BF16)
        new = update(narrow_in[0, member], narrow_in[1, member], narrow_in[2, member]).astype(BF16)
        out[HALF : HALF + R, :] = new[:, :HD]
        out[HALF + R :, :] = new[:, HD:]


def new_factors(place, wide, narrow):
    out = jax.ShapeDtypeStruct((HALF + 2 * R, 2 * R), BF16)
    return pl.pallas_call(
        factor_kernel,
        out_shape=(out, out),
        in_specs=[smem()] + [pl.BlockSpec(memory_space=pl.ANY)] * 6,
        out_specs=(vmem(), vmem()),
        scratch_shapes=[
            pltpu.VMEM((3, 2, R, SW), F32),
            pltpu.VMEM((3, 2, R, QW), F32),
            pltpu.VMEM((SW + 96, 2 * R), F32),
            pltpu.SemaphoreType.DMA((6,)),
        ],
        compiler_params=pltpu.CompilerParams(vmem_limit_bytes=56 * MIB),
        cost_estimate=pl.CostEstimate(flops=0, bytes_accessed=MIB, transcendentals=0),
    )(place, *wide, *narrow)


def both_halves(nq):
    nq = nq.astype(F32)
    return jnp.concatenate([nq[:R], nq[R:]], axis=1)


def merge_query_kernel(place_ref, own_ref, other_ref, wq_ref, out_ref, b_q):
    x, z, c = place_ref[0], place_ref[1], place_ref[2]
    zeros = jnp.zeros((R, QW), F32)

    @pl.when(c == 0)
    def _():
        b_q[...] = jnp.concatenate([both_halves(own_ref[0, NZ * HALF :]), zeros], axis=0).astype(BF16)

    @pl.when(c == 1)
    def _():
        b_q[...] = jnp.concatenate([both_halves(other_ref[0, NZ * HALF :]), zeros], axis=0).astype(BF16)

    factor = b_q[...]
    for core, pieces in ((c, own_ref), (1 - c, other_ref)):
        for jx in range(NX):
            for jz in range(NZ):
                there = lax.rem(z + jz, NZ)
                source = (there * NX + lax.rem(x + jx, NX)) * 2 + core
                target = (jx * NZ + there) * 2 + core
                piece = pieces[jx, jz * HALF : (jz + 1) * HALF]
                delta = jnp.dot(piece, factor, preferred_element_type=F32)
                out_ref[target] = (wq_ref[source].astype(F32) + delta).astype(BF16)


def merge_query(place, own, other, w_query):
    out = pl.pallas_call(
        merge_query_kernel,
        out_shape=jax.ShapeDtypeStruct((2 * NX * NZ, HALF, QW), BF16),
        in_specs=[smem()] + [vmem()] * 3,
        out_specs=vmem(),
        scratch_shapes=[pltpu.VMEM((2 * R, QW), BF16)],
        compiler_params=pltpu.CompilerParams(vmem_limit_bytes=12 * MIB),
        cost_estimate=pl.CostEstimate(flops=2 * D * QW * 128, bytes_accessed=6 * MIB, transcendentals=0),
    )(place, own, other, w_query.reshape(2 * NX * NZ, HALF, QW))
    return out.reshape(NX, BW, QW)


def merge_out_kernel(place_ref, own_ref, other_ref, home_ref, *refs):
    z, c = place_ref[1], place_ref[2]
    mine, theirs = refs[0:3], refs[3:6]
    out_ref, wide, small, delta = refs[6:]
    for core, pieces in ((c, own_ref), (1 - c, other_ref)):
        for jz in range(NZ):
            wide[lax.rem(z + jz, NZ) * 2 + core] = pieces[0, jz * HALF : (jz + 1) * HALF]
        small[core] = pieces[:, NZ * HALF :]
    b_o = wide[...].reshape(BW, 2 * R)
    zeros = jnp.zeros((R, QW), F32)
    for j in range(NX):
        a_o = jnp.concatenate([zeros, both_halves(small[1, j])], axis=0).T.astype(BF16)
        change = lax.dot_general(a_o, b_o, (((1,), (1,)), ((), ())), preferred_element_type=F32)
        change = change.reshape(2, QW // 2, BW)
        if j == 0:
            out_ref[0] = (home_ref[...].astype(F32).reshape(2, QW // 2, BW) + change).astype(BF16)
        else:
            delta[...] = change
            out_ref[j, c] = (mine[j - 1][...].astype(F32) + delta[c]).astype(BF16)
            out_ref[j, 1 - c] = (theirs[j - 1][...].astype(F32) + delta[1 - c]).astype(BF16)


def merge_out(place, own, other, home, mine, theirs):
    out = pl.pallas_call(
        merge_out_kernel,
        out_shape=jax.ShapeDtypeStruct((NX, 2, QW // 2, BW), BF16),
        in_specs=[smem()] + [vmem()] * 9,
        out_specs=vmem(),
        scratch_shapes=[
            pltpu.VMEM((2 * NZ, HALF, 2 * R), BF16),
            pltpu.VMEM((2, NX, 2 * R, 2 * R), BF16),
            pltpu.VMEM((2, QW // 2, BW), F32),
        ],
        compiler_params=pltpu.CompilerParams(vmem_limit_bytes=14 * MIB),
        cost_estimate=pl.CostEstimate(flops=2 * D * QW * 128, bytes_accessed=6 * MIB, transcendentals=0),
    )(place, own, other, home, *mine, *theirs)
    return out.reshape(NX * QW, BW)


def soft(score):
    return jnp.exp(SOFT_CAP * jnp.tanh(score * (SCORE_SCALE / SOFT_CAP)))


def step_kernel(turn, stream, *refs):
    refs = list(refs)

    def take(count):
        taken = refs[:count]
        del refs[:count]
        return taken

    start = BOUNDS[stream]
    count = BOUNDS[stream + 1] - start
    mine = slice(start, start + count)
    if turn == 0:
        held = [ref[mine, :].astype(F32) for ref in take(NX)]
    else:
        branch = [ref[...].astype(F32) for ref in take(NX)]
        (res_ref,) = take(1)
    post_ref, pre_ref, len_ref, cos_ref, sin_ref = take(5)
    old = take(2 * turn)
    wq, wkv, kc, vc = take(4)
    res_out, att_out, fk_out, fv_out = take(4)
    if turn > 0:
        square = sum(jnp.sum(b * b, axis=1, keepdims=True) for b in branch)
        scale = lax.rsqrt(square * (1.0 / D) + EPSILON)
        held = [
            (res_ref[j].astype(F32) + branch[j] * scale * post_ref[j : j + 1, :]).astype(BF16).astype(F32)
            for j in range(NX)
        ]
    square = sum(jnp.sum(r * r, axis=1, keepdims=True) for r in held)
    scale = lax.rsqrt(square * (1.0 / D) + EPSILON)
    q = jnp.zeros((count, QW), F32)
    kv = jnp.zeros((count, 2 * HD), F32)
    for j in range(NX):
        res_out[j] = held[j].astype(BF16)
        normed = (held[j] * scale * pre_ref[j : j + 1, :]).astype(BF16)
        q = q + jnp.dot(normed, wq[j], preferred_element_type=F32)
        kv = kv + jnp.dot(normed, wkv[j], preferred_element_type=F32)
    cosine = cos_ref[turn, mine, :]
    sine = sin_ref[turn, mine, :]

    def rope(matrix):
        return (matrix * cosine + pltpu.roll(matrix, HD // 2, 1) * sine).astype(BF16)

    q0 = rope(q[:, :HD]).astype(F32)
    q1 = rope(q[:, HD:]).astype(F32)
    fresh_k = rope(kv[:, :HD])
    fresh_v = kv[:, HD:].astype(BF16)
    fk_out[...] = fresh_k
    fv_out[...] = fresh_v
    keys = [old[2 * s][...].astype(F32) for s in range(turn)] + [fresh_k.astype(F32)]
    values = [old[2 * s + 1][...].astype(F32) for s in range(turn)] + [fresh_v.astype(F32)]
    new0 = [soft(jnp.sum(q0 * k, axis=1, keepdims=True)) for k in keys]
    new1 = [soft(jnp.sum(q1 * k, axis=1, keepdims=True)) for k in keys]
    new_sum0 = sum(new0[1:], new0[0])
    new_sum1 = sum(new1[1:], new1[0])
    column = lax.broadcasted_iota(jnp.int32, (16, 8 * CACHE), 1)
    low = lax.rem(lax.broadcasted_iota(jnp.int32, (16, 1), 0), 8) * CACHE
    weights = []
    inverse = []
    for i in range(count // 8):
        here = slice(8 * i, 8 * i + 8)
        there = slice(start + 8 * i, start + 8 * i + 8)
        queries = jnp.concatenate([q0[here], q1[here]], axis=0).astype(BF16)
        block = kc[there].reshape(8 * CACHE, HD)
        score = lax.dot_general(queries, block, (((1,), (1,)), ((), ())), preferred_element_type=F32)
        length = len_ref[there]
        length = jnp.concatenate([length, length], axis=0)
        mask = (column >= low) & (column < low + length)
        value = jnp.where(mask, soft(score), 0.0)
        total = jnp.sum(value, axis=1, keepdims=True)
        total = total + jnp.concatenate([new_sum0[here], new_sum1[here]], axis=0)
        inv = 1.0 / total
        inverse.append(inv)
        weights.append((value * inv).astype(BF16))
    inv0 = jnp.concatenate([inv[:8] for inv in inverse], axis=0)
    inv1 = jnp.concatenate([inv[8:] for inv in inverse], axis=0)

    def recent(new, inv):
        total = None
        for w, v in zip(new, values):
            term = (w * inv).astype(BF16).astype(F32) * v
            total = term if total is None else total + term
        return total

    add0 = recent(new0, inv0)
    add1 = recent(new1, inv1)
    got0 = []
    got1 = []
    for i in range(count // 8):
        there = slice(start + 8 * i, start + 8 * i + 8)
        block = vc[there].reshape(8 * CACHE, HD)
        summed = jnp.dot(weights[i], block, preferred_element_type=F32)
        got0.append(summed[:8])
        got1.append(summed[8:])
    att_out[:, :HD] = (jnp.concatenate(got0, axis=0) + add0).astype(BF16)
    att_out[:, HD:] = (jnp.concatenate(got1, axis=0) + add1).astype(BF16)


def step(turn, stream, blocks, residual, post, pre, lengths, cosine, sine, old, w_query, w_kv, keys, values):
    rows = BOUNDS[stream + 1] - BOUNDS[stream]
    fresh = jax.ShapeDtypeStruct((rows, HD), BF16)
    state = list(blocks) + ([] if turn == 0 else [residual])
    args = state + [post, pre, lengths, cosine, sine] + old + [w_query, w_kv, keys, values]
    return pl.pallas_call(
        functools.partial(step_kernel, turn, stream),
        out_shape=(
            jax.ShapeDtypeStruct((NX, rows, BW), BF16),
            jax.ShapeDtypeStruct((rows, QW), BF16),
            fresh,
            fresh,
        ),
        in_specs=[vmem()] * len(args),
        out_specs=(vmem(),) * 4,
        compiler_params=pltpu.CompilerParams(vmem_limit_bytes=14 * MIB),
        cost_estimate=pl.CostEstimate(flops=2 * rows * D * 512, bytes_accessed=10 * MIB, transcendentals=0),
    )(*args)


def project_kernel(a0, a1, a2, a3, w_ref, *outs):
    attended = jnp.concatenate([a0[...], a1[...], a2[...], a3[...]], axis=1)
    partial = jnp.dot(attended, w_ref[...], preferred_element_type=F32).astype(BF16)
    for s, out in enumerate(outs):
        out[...] = partial[BOUNDS[s] : BOUNDS[s + 1]]


def project(attended, w_out):
    return pl.pallas_call(
        project_kernel,
        out_shape=[jax.ShapeDtypeStruct((b - a, BW), BF16) for a, b in zip(BOUNDS, BOUNDS[1:])],
        in_specs=[vmem()] * 5,
        out_specs=[vmem()] * STREAMS,
        compiler_params=pltpu.CompilerParams(vmem_limit_bytes=14 * MIB),
        cost_estimate=pl.CostEstimate(flops=2 * ROWS * BW * 1024, bytes_accessed=3 * MIB, transcendentals=0),
    )(*attended, w_out)


def final_kernel(place_ref, *refs):
    residual, sums = refs[:STREAMS], refs[STREAMS : 2 * STREAMS]
    squares = refs[2 * STREAMS : 2 * STREAMS + NX]
    post_ref, out_ref, pieces = refs[2 * STREAMS + NX :]
    square = (squares[0][...] + squares[1][...]) + (squares[2][...] + squares[3][...])
    square = jnp.concatenate([square, jnp.zeros((1, 128 - ROWS), F32)], axis=1)
    square = jnp.broadcast_to(square, (128, 128)).T[:ROWS, :1]
    scale = lax.rsqrt(square * (1.0 / D) + EPSILON)
    for s in range(STREAMS):
        rows = slice(BOUNDS[s], BOUNDS[s + 1])
        final = residual[s][0].astype(F32) + sums[s][...] * scale[rows] * post_ref[:1, :]
        final = final.astype(BF16)
        for z in range(NZ):
            pieces[z, rows, :] = final[:, z * SW : (z + 1) * SW]
    out_ref[...] = pieces[place_ref[1]]


def finish(place, residual, sums, squares, post):
    return pl.pallas_call(
        final_kernel,
        out_shape=jax.ShapeDtypeStruct((ROWS, SW), BF16),
        in_specs=[smem()] + [vmem()] * (2 * STREAMS + NX + 1),
        out_specs=vmem(),
        scratch_shapes=[pltpu.VMEM((NZ, ROWS, SW), BF16)],
        compiler_params=pltpu.CompilerParams(vmem_limit_bytes=8 * MIB),
        cost_estimate=pl.CostEstimate(flops=0, bytes_accessed=MIB, transcendentals=0),
    )(place, *residual, *sums, *squares, post)


def add_up(blocks):
    first, *rest = [b.astype(F32) for b in blocks]
    return sum(rest, first)


def body(
    hidden,
    cache_len,
    layer_index,
    pre_gain,
    post_gain,
    w_query,
    w_key,
    w_value,
    w_out,
    cache_keys,
    cache_values,
    wide_factors,
    narrow_factors,
    wide_momentum,
    narrow_momentum,
    wide_gradient,
    narrow_gradient,
):
    tensor = lax.axis_index("tensor")
    group = lax.axis_index("group")
    x = tensor % NX
    z = tensor // NX
    core = group % 2
    layers_here = wide_factors.shape[0]
    owner = layer_index[0] // layers_here
    slot = layer_index[0] % layers_here
    place = jnp.stack([x, z, core, owner == group, slot]).astype(jnp.int32)
    lengths = cache_len[:, None]
    place = after(place, lengths)

    wide = [wide_factors, wide_momentum, wide_gradient]
    narrow = [narrow_factors, narrow_momentum, narrow_gradient]
    mine, theirs = new_factors(place, wide, narrow)
    mine = mine + send_core(theirs)

    pieces = gather_z(hidden)
    block = join(place, pieces)
    mine = mine + send_y(mine, 1) + send_y(mine, 2) + send_y(mine, 3)
    parts = split(after(place, mine), w_out)
    mine = after(mine + send_w(mine), (block, parts))
    blocks = gather_x(block)
    w_kv, post, pre = arrange(after(place, mine), w_key, w_value, post_gain, pre_gain)
    cache_len = after(cache_len, mine)

    frequency = ROPE_BASE ** (-jnp.arange(HD // 2, dtype=F32) * 2.0 / HD)
    position = (cache_len[None, :] + jnp.arange(STEPS)[:, None]).astype(F32)
    angles = position[:, :, None] * frequency
    cosine = jnp.cos(angles)
    sine = jnp.sin(angles)
    cosine = jnp.concatenate([cosine, cosine], axis=-1)
    sine = jnp.concatenate([-sine, sine], axis=-1)

    column = jnp.concatenate(gather_z(mine[:HALF]) + [mine[HALF:]])
    column = after(column, blocks)
    own = jnp.stack(after(gather_x(column), (w_kv, post, pre, cosine, sine)))
    other = send_core(own)

    out_mine = [send_x(after(parts[j], own), -j) for j in range(1, NX)]
    merged_query = merge_query(place, own, other, w_query)

    blocks = [blocks] * STREAMS
    residual = [None] * STREAMS
    old = [[] for _ in range(STREAMS)]
    sums = [None] * STREAMS
    for turn in range(STEPS):
        attended = [None] * STREAMS
        for s in range(STREAMS):
            residual[s], attended[s], fresh_k, fresh_v = step(
                turn, s, blocks[s], residual[s], post, pre, lengths, cosine, sine, old[s],
                merged_query, w_kv, cache_keys, cache_values,
            )
            old[s] = old[s] + [fresh_k, fresh_v]
        if turn == 0:
            out_theirs = [send_core(after(v, attended)) for v in out_mine]
            merged_out = merge_out(place, own, other, parts[0], out_mine, out_theirs)
        partial = project(gather_x(jnp.concatenate(attended)), merged_out)
        for s in range(STREAMS):
            sums[s] = add_up(gather_z(partial[s]))
            if turn < STEPS - 1:
                blocks[s] = gather_x(sums[s].astype(BF16))

    squares = gather_x(jnp.concatenate([jnp.sum(v * v, axis=1) for v in sums])[None])
    return finish(place, residual, sums, squares, post)


def solution(mesh):
    rows = P("group", "tensor")
    columns = P(None, "tensor")
    cache = P("group", None, "tensor")
    state = P("group", None, None, "tensor")
    in_specs = (
        rows,
        P("group"),
        P(),
        P(),
        P(),
        columns,
        columns,
        columns,
        P("tensor", None),
        cache,
        cache,
    ) + (state,) * 6
    return jax.shard_map(body, mesh=mesh, in_specs=in_specs, out_specs=rows, check_vma=False)
```

```python
import functools

import jax
import jax.numpy as jnp
from jax import lax
from jax.experimental import pallas as pl
from jax.experimental.pallas import tpu as pltpu
from jax.sharding import PartitionSpec as P

D = 4608
HQ = 32
HD = 128
R = 64
ROWS = 96
CACHE = 96
STEPS = 4
QW = 256
NX = 4
NZ = 4
SW = D // (NX * NZ)
BW = D // NX
HALF = SW // 2
BOUNDS = (0, 48, 96)
STREAMS = len(BOUNDS) - 1

LEARN_RATE = 0.25
MOMENTUM_DECAY = 0.9
EPSILON = 1e-06
SOFT_CAP = 50.0
ROPE_BASE = 10000.0
SCORE_SCALE = (D / HQ) ** (-0.5)

F32 = jnp.float32
BF16 = jnp.bfloat16
MIB = 2**20


def send_x(value, shift):
    pairs = [(z * NX + x, z * NX + (x + shift) % NX) for z in range(NZ) for x in range(NX)]
    return lax.ppermute(value, "tensor", pairs)


def send_z(value, shift):
    pairs = [(z * NX + x, ((z + shift) % NZ) * NX + x) for z in range(NZ) for x in range(NX)]
    return lax.ppermute(value, "tensor", pairs)


def send_y(value, shift):
    pairs = [
        (w * 8 + y * 2 + c, w * 8 + ((y + shift) % 4) * 2 + c)
        for w in range(2)
        for y in range(4)
        for c in range(2)
    ]
    return lax.ppermute(value, "group", pairs)


def send_w(value):
    return lax.ppermute(value, "group", [(g, (g + 8) % 16) for g in range(16)])


def send_core(value):
    return lax.ppermute(value, "group", [(g, g ^ 1) for g in range(16)])


def gather_x(value):
    return [value] + [send_x(value, -j) for j in range(1, NX)]


def gather_z(value):
    return [value] + [send_z(value, -j) for j in range(1, NZ)]


def after(value, earlier):
    return lax.optimization_barrier((value, earlier))[0]


def smem():
    return pl.BlockSpec(memory_space=pltpu.SMEM)


def vmem():
    return pl.BlockSpec(memory_space=pltpu.VMEM)


def by_x(array, x):
    return jnp.concatenate([array[:, (z * NX + x) * SW : (z * NX + x + 1) * SW] for z in range(NZ)], axis=1)


def arrange_kernel(place_ref, wk_ref, wv_ref, post_ref, pre_ref, out_ref, post_out, pre_out):
    x = place_ref[0]
    for j in range(NX):
        for z in range(NZ):
            t = z * NX + lax.rem(x + j, NX)
            out_ref[j * NZ + z, :, :HD] = wk_ref[t]
            out_ref[j * NZ + z, :, HD:] = wv_ref[t]
    for there in range(NX):
        j = lax.rem(there - x + NX, NX)
        post_out[j] = by_x(post_ref[...], there)
        pre_out[j] = by_x(pre_ref[...], there)


def arrange(place, w_key, w_value, post_gain, pre_gain):
    gain = jax.ShapeDtypeStruct((NX, 1, BW), F32)
    out, post, pre = pl.pallas_call(
        arrange_kernel,
        out_shape=(jax.ShapeDtypeStruct((NX * NZ, SW, 2 * HD), BF16), gain, gain),
        in_specs=[smem()] + [vmem()] * 4,
        out_specs=(vmem(),) * 3,
        compiler_params=pltpu.CompilerParams(vmem_limit_bytes=14 * MIB),
        cost_estimate=pl.CostEstimate(flops=0, bytes_accessed=5 * MIB, transcendentals=0),
    )(place, w_key.reshape(NX * NZ, SW, HD), w_value.reshape(NX * NZ, SW, HD), post_gain[None], pre_gain[None])
    return out.reshape(NX, BW, 2 * HD), post.reshape(NX, BW), pre.reshape(NX, BW)


def split_kernel(place_ref, w_ref, home_out, o1, o2, o3, rolled):
    x, c = place_ref[0], place_ref[2]
    for there in range(NX):
        piece = by_x(w_ref[...], there)
        j = lax.rem(x - there + NX, NX)
        rolled[j, 0] = piece[: QW // 2]
        rolled[j, 1] = piece[QW // 2 :]
    home_out[...] = rolled[0].reshape(QW, BW)
    for j, out in enumerate((o1, o2, o3)):
        out[...] = rolled[j + 1, c]


def split(place, w_out):
    half = jax.ShapeDtypeStruct((QW // 2, BW), BF16)
    return pl.pallas_call(
        split_kernel,
        out_shape=(jax.ShapeDtypeStruct((QW, BW), BF16), half, half, half),
        in_specs=[smem(), vmem()],
        out_specs=(vmem(),) * NX,
        scratch_shapes=[pltpu.VMEM((NX, 2, QW // 2, BW), BF16)],
        compiler_params=pltpu.CompilerParams(vmem_limit_bytes=12 * MIB),
        cost_estimate=pl.CostEstimate(flops=0, bytes_accessed=5 * MIB, transcendentals=0),
    )(place, w_out)


def join_kernel(place_ref, p0, p1, p2, p3, out_ref, rolled):
    z = place_ref[1]
    for j, piece in enumerate((p0, p1, p2, p3)):
        rolled[lax.rem(z + j, NZ)] = piece[...]
    out_ref[...] = jnp.concatenate([rolled[i] for i in range(NZ)], axis=1)


def join(place, pieces):
    return pl.pallas_call(
        join_kernel,
        out_shape=jax.ShapeDtypeStruct((ROWS, BW), BF16),
        in_specs=[smem()] + [vmem()] * NZ,
        out_specs=vmem(),
        scratch_shapes=[pltpu.VMEM((NZ, ROWS, SW), BF16)],
        compiler_params=pltpu.CompilerParams(vmem_limit_bytes=4 * MIB),
        cost_estimate=pl.CostEstimate(flops=0, bytes_accessed=MIB // 2, transcendentals=0),
    )(place, *pieces)


def factor_kernel(place_ref, *refs):
    wide_hbm, narrow_hbm = refs[0:3], refs[3:6]
    mine_out, theirs_out = refs[6:8]
    wide_in, narrow_in, wide, sems = refs[8:]
    c, owned, slot = place_ref[2], place_ref[3], place_ref[4]
    copies = []
    for i in range(3):
        copies.append(pltpu.make_async_copy(wide_hbm[i].at[slot], wide_in.at[i], sems.at[i]))
        copies.append(pltpu.make_async_copy(narrow_hbm[i].at[slot], narrow_in.at[i], sems.at[3 + i]))
    for copy in copies:
        copy.start()
    for copy in copies:
        copy.wait()

    def update(old, momentum, gradient):
        new = old - LEARN_RATE * (MOMENTUM_DECAY * momentum + gradient)
        return jnp.where(owned == 1, new, 0.0)

    new = update(wide_in[0], wide_in[1], wide_in[2]).reshape(2 * R, SW)
    new = jnp.concatenate([new, jnp.zeros((2 * R, 96), F32)], axis=1)
    wide[...] = new.T
    for out, member in ((mine_out, c), (theirs_out, 1 - c)):
        out[:HALF, :] = wide[pl.ds(pl.multiple_of(member * HALF, 8), HALF), :].astype(BF16)
        new = update(narrow_in[0, member], narrow_in[1, member], narrow_in[2, member]).astype(BF16)
        out[HALF : HALF + R, :] = new[:, :HD]
        out[HALF + R :, :] = new[:, HD:]


def new_factors(place, wide, narrow):
    out = jax.ShapeDtypeStruct((HALF + 2 * R, 2 * R), BF16)
    return pl.pallas_call(
        factor_kernel,
        out_shape=(out, out),
        in_specs=[smem()] + [pl.BlockSpec(memory_space=pl.ANY)] * 6,
        out_specs=(vmem(), vmem()),
        scratch_shapes=[
            pltpu.VMEM((3, 2, R, SW), F32),
            pltpu.VMEM((3, 2, R, QW), F32),
            pltpu.VMEM((SW + 96, 2 * R), F32),
            pltpu.SemaphoreType.DMA((6,)),
        ],
        compiler_params=pltpu.CompilerParams(vmem_limit_bytes=56 * MIB),
        cost_estimate=pl.CostEstimate(flops=0, bytes_accessed=MIB, transcendentals=0),
    )(place, *wide, *narrow)


def both_halves(nq):
    nq = nq.astype(F32)
    return jnp.concatenate([nq[:R], nq[R:]], axis=1)


def merge_query_kernel(place_ref, own_ref, other_ref, wq_ref, out_ref, b_q):
    x, z, c = place_ref[0], place_ref[1], place_ref[2]
    zeros = jnp.zeros((R, QW), F32)

    @pl.when(c == 0)
    def _():
        b_q[...] = jnp.concatenate([both_halves(own_ref[0, NZ * HALF :]), zeros], axis=0).astype(BF16)

    @pl.when(c == 1)
    def _():
        b_q[...] = jnp.concatenate([both_halves(other_ref[0, NZ * HALF :]), zeros], axis=0).astype(BF16)

    factor = b_q[...]
    for core, pieces in ((c, own_ref), (1 - c, other_ref)):
        for jx in range(NX):
            for jz in range(NZ):
                there = lax.rem(z + jz, NZ)
                source = (there * NX + lax.rem(x + jx, NX)) * 2 + core
                target = (jx * NZ + there) * 2 + core
                piece = pieces[jx, jz * HALF : (jz + 1) * HALF]
                delta = jnp.dot(piece, factor, preferred_element_type=F32)
                out_ref[target] = (wq_ref[source].astype(F32) + delta).astype(BF16)


def merge_query(place, own, other, w_query):
    out = pl.pallas_call(
        merge_query_kernel,
        out_shape=jax.ShapeDtypeStruct((2 * NX * NZ, HALF, QW), BF16),
        in_specs=[smem()] + [vmem()] * 3,
        out_specs=vmem(),
        scratch_shapes=[pltpu.VMEM((2 * R, QW), BF16)],
        compiler_params=pltpu.CompilerParams(vmem_limit_bytes=12 * MIB),
        cost_estimate=pl.CostEstimate(flops=2 * D * QW * 128, bytes_accessed=6 * MIB, transcendentals=0),
    )(place, own, other, w_query.reshape(2 * NX * NZ, HALF, QW))
    return out.reshape(NX, BW, QW)


def merge_out_kernel(place_ref, own_ref, other_ref, home_ref, *refs):
    z, c = place_ref[1], place_ref[2]
    mine, theirs = refs[0:3], refs[3:6]
    out_ref, wide, small, delta = refs[6:]
    for core, pieces in ((c, own_ref), (1 - c, other_ref)):
        for jz in range(NZ):
            wide[lax.rem(z + jz, NZ) * 2 + core] = pieces[0, jz * HALF : (jz + 1) * HALF]
        small[core] = pieces[:, NZ * HALF :]
    b_o = wide[...].reshape(BW, 2 * R)
    zeros = jnp.zeros((R, QW), F32)
    for j in range(NX):
        a_o = jnp.concatenate([zeros, both_halves(small[1, j])], axis=0).T.astype(BF16)
        change = lax.dot_general(a_o, b_o, (((1,), (1,)), ((), ())), preferred_element_type=F32)
        change = change.reshape(2, QW // 2, BW)
        if j == 0:
            out_ref[0] = (home_ref[...].astype(F32).reshape(2, QW // 2, BW) + change).astype(BF16)
        else:
            delta[...] = change
            out_ref[j, c] = (mine[j - 1][...].astype(F32) + delta[c]).astype(BF16)
            out_ref[j, 1 - c] = (theirs[j - 1][...].astype(F32) + delta[1 - c]).astype(BF16)


def merge_out(place, own, other, home, mine, theirs):
    out = pl.pallas_call(
        merge_out_kernel,
        out_shape=jax.ShapeDtypeStruct((NX, 2, QW // 2, BW), BF16),
        in_specs=[smem()] + [vmem()] * 9,
        out_specs=vmem(),
        scratch_shapes=[
            pltpu.VMEM((2 * NZ, HALF, 2 * R), BF16),
            pltpu.VMEM((2, NX, 2 * R, 2 * R), BF16),
            pltpu.VMEM((2, QW // 2, BW), F32),
        ],
        compiler_params=pltpu.CompilerParams(vmem_limit_bytes=14 * MIB),
        cost_estimate=pl.CostEstimate(flops=2 * D * QW * 128, bytes_accessed=6 * MIB, transcendentals=0),
    )(place, own, other, home, *mine, *theirs)
    return out.reshape(NX * QW, BW)


def soft(score):
    return jnp.exp(SOFT_CAP * jnp.tanh(score * (SCORE_SCALE / SOFT_CAP)))


def step_kernel(turn, start, stop, *refs):
    refs = list(refs)

    def take(count):
        taken = refs[:count]
        del refs[:count]
        return taken

    count = stop - start
    mine = slice(start, stop)

    def own_rows(ref):
        return ref[mine, :] if ref.shape[0] == ROWS else ref[...]

    if turn == 0:
        held = [ref[mine, :].astype(F32) for ref in take(NX)]
    else:
        branch = [ref[...].astype(F32) for ref in take(NX)]
        (res_ref,) = take(1)
    post_ref, pre_ref, len_ref, cos_ref, sin_ref = take(5)
    old = take(2 * turn)
    wq, wkv, kc, vc = take(4)
    res_out, att_out, fk_out, fv_out = take(4)
    if turn > 0:
        square = sum(jnp.sum(b * b, axis=1, keepdims=True) for b in branch)
        scale = lax.rsqrt(square * (1.0 / D) + EPSILON)
        held = [
            (own_rows(res_ref.at[j]).astype(F32) + branch[j] * scale * post_ref[j : j + 1, :]).astype(BF16).astype(F32)
            for j in range(NX)
        ]
    square = sum(jnp.sum(r * r, axis=1, keepdims=True) for r in held)
    scale = lax.rsqrt(square * (1.0 / D) + EPSILON)
    q = jnp.zeros((count, QW), F32)
    kv = jnp.zeros((count, 2 * HD), F32)
    for j in range(NX):
        res_out[j] = held[j].astype(BF16)
        normed = (held[j] * scale * pre_ref[j : j + 1, :]).astype(BF16)
        q = q + jnp.dot(normed, wq[j], preferred_element_type=F32)
        kv = kv + jnp.dot(normed, wkv[j], preferred_element_type=F32)
    cosine = cos_ref[turn, mine, :]
    sine = sin_ref[turn, mine, :]

    def rope(matrix):
        return (matrix * cosine + pltpu.roll(matrix, HD // 2, 1) * sine).astype(BF16)

    q0 = rope(q[:, :HD]).astype(F32)
    q1 = rope(q[:, HD:]).astype(F32)
    fresh_k = rope(kv[:, :HD])
    fresh_v = kv[:, HD:].astype(BF16)
    fk_out[...] = fresh_k
    fv_out[...] = fresh_v
    keys = [own_rows(old[2 * s]).astype(F32) for s in range(turn)] + [fresh_k.astype(F32)]
    values = [own_rows(old[2 * s + 1]).astype(F32) for s in range(turn)] + [fresh_v.astype(F32)]
    new0 = [soft(jnp.sum(q0 * k, axis=1, keepdims=True)) for k in keys]
    new1 = [soft(jnp.sum(q1 * k, axis=1, keepdims=True)) for k in keys]
    new_sum0 = sum(new0[1:], new0[0])
    new_sum1 = sum(new1[1:], new1[0])
    column = lax.broadcasted_iota(jnp.int32, (16, 8 * CACHE), 1)
    low = lax.rem(lax.broadcasted_iota(jnp.int32, (16, 1), 0), 8) * CACHE
    weights = []
    inverse = []
    for i in range(count // 8):
        here = slice(8 * i, 8 * i + 8)
        there = slice(start + 8 * i, start + 8 * i + 8)
        queries = jnp.concatenate([q0[here], q1[here]], axis=0).astype(BF16)
        block = kc[there].reshape(8 * CACHE, HD)
        score = lax.dot_general(queries, block, (((1,), (1,)), ((), ())), preferred_element_type=F32)
        length = len_ref[there]
        length = jnp.concatenate([length, length], axis=0)
        mask = (column >= low) & (column < low + length)
        value = jnp.where(mask, soft(score), 0.0)
        total = jnp.sum(value, axis=1, keepdims=True)
        total = total + jnp.concatenate([new_sum0[here], new_sum1[here]], axis=0)
        inv = 1.0 / total
        inverse.append(inv)
        weights.append((value * inv).astype(BF16))
    inv0 = jnp.concatenate([inv[:8] for inv in inverse], axis=0)
    inv1 = jnp.concatenate([inv[8:] for inv in inverse], axis=0)

    def recent(new, inv):
        total = None
        for w, v in zip(new, values):
            term = (w * inv).astype(BF16).astype(F32) * v
            total = term if total is None else total + term
        return total

    add0 = recent(new0, inv0)
    add1 = recent(new1, inv1)
    got0 = []
    got1 = []
    for i in range(count // 8):
        there = slice(start + 8 * i, start + 8 * i + 8)
        block = vc[there].reshape(8 * CACHE, HD)
        summed = jnp.dot(weights[i], block, preferred_element_type=F32)
        got0.append(summed[:8])
        got1.append(summed[8:])
    att_out[:, :HD] = (jnp.concatenate(got0, axis=0) + add0).astype(BF16)
    att_out[:, HD:] = (jnp.concatenate(got1, axis=0) + add1).astype(BF16)


def step(turn, start, stop, blocks, residual, post, pre, lengths, cosine, sine, old, w_query, w_kv, keys, values):
    rows = stop - start
    fresh = jax.ShapeDtypeStruct((rows, HD), BF16)
    state = list(blocks) + ([] if turn == 0 else [residual])
    args = state + [post, pre, lengths, cosine, sine] + old + [w_query, w_kv, keys, values]
    return pl.pallas_call(
        functools.partial(step_kernel, turn, start, stop),
        out_shape=(
            jax.ShapeDtypeStruct((NX, rows, BW), BF16),
            jax.ShapeDtypeStruct((rows, QW), BF16),
            fresh,
            fresh,
        ),
        in_specs=[vmem()] * len(args),
        out_specs=(vmem(),) * 4,
        compiler_params=pltpu.CompilerParams(vmem_limit_bytes=14 * MIB),
        cost_estimate=pl.CostEstimate(flops=2 * rows * D * 512, bytes_accessed=10 * MIB, transcendentals=0),
    )(*args)


def project_kernel(a0, a1, a2, a3, w_ref, *outs):
    attended = jnp.concatenate([a0[...], a1[...], a2[...], a3[...]], axis=1)
    partial = jnp.dot(attended, w_ref[...], preferred_element_type=F32).astype(BF16)
    begin = 0
    for out in outs:
        out[...] = partial[begin : begin + out.shape[0]]
        begin += out.shape[0]


def project(attended, w_out, bounds):
    return pl.pallas_call(
        project_kernel,
        out_shape=[jax.ShapeDtypeStruct((b - a, BW), BF16) for a, b in zip(bounds, bounds[1:])],
        in_specs=[vmem()] * 5,
        out_specs=[vmem()] * (len(bounds) - 1),
        compiler_params=pltpu.CompilerParams(vmem_limit_bytes=14 * MIB),
        cost_estimate=pl.CostEstimate(flops=2 * ROWS * BW * 1024, bytes_accessed=3 * MIB, transcendentals=0),
    )(*attended, w_out)


def final_kernel(place_ref, *refs):
    residual, sums = refs[:STREAMS], refs[STREAMS]
    squares = refs[STREAMS + 1 : STREAMS + 1 + NX]
    post_ref, out_ref, pieces = refs[STREAMS + 1 + NX :]
    square = (squares[0][...] + squares[1][...]) + (squares[2][...] + squares[3][...])
    square = jnp.concatenate([square, jnp.zeros((1, 128 - ROWS), F32)], axis=1)
    square = jnp.broadcast_to(square, (128, 128)).T[:ROWS, :1]
    scale = lax.rsqrt(square * (1.0 / D) + EPSILON)
    for s in range(STREAMS):
        rows = slice(BOUNDS[s], BOUNDS[s + 1])
        final = residual[s][0].astype(F32) + sums[rows, :] * scale[rows] * post_ref[:1, :]
        final = final.astype(BF16)
        for z in range(NZ):
            pieces[z, rows, :] = final[:, z * SW : (z + 1) * SW]
    out_ref[...] = pieces[place_ref[1]]


def finish(place, residual, sums, squares, post):
    return pl.pallas_call(
        final_kernel,
        out_shape=jax.ShapeDtypeStruct((ROWS, SW), BF16),
        in_specs=[smem()] + [vmem()] * (STREAMS + NX + 2),
        out_specs=vmem(),
        scratch_shapes=[pltpu.VMEM((NZ, ROWS, SW), BF16)],
        compiler_params=pltpu.CompilerParams(vmem_limit_bytes=8 * MIB),
        cost_estimate=pl.CostEstimate(flops=0, bytes_accessed=MIB, transcendentals=0),
    )(place, *residual, sums, *squares, post)


def add_up(blocks):
    first, *rest = [b.astype(F32) for b in blocks]
    return sum(rest, first)


def body(
    hidden,
    cache_len,
    layer_index,
    pre_gain,
    post_gain,
    w_query,
    w_key,
    w_value,
    w_out,
    cache_keys,
    cache_values,
    wide_factors,
    narrow_factors,
    wide_momentum,
    narrow_momentum,
    wide_gradient,
    narrow_gradient,
):
    tensor = lax.axis_index("tensor")
    group = lax.axis_index("group")
    x = tensor % NX
    z = tensor // NX
    core = group % 2
    layers_here = wide_factors.shape[0]
    owner = layer_index[0] // layers_here
    slot = layer_index[0] % layers_here
    place = jnp.stack([x, z, core, owner == group, slot]).astype(jnp.int32)
    lengths = cache_len[:, None]
    place = after(place, lengths)

    wide = [wide_factors, wide_momentum, wide_gradient]
    narrow = [narrow_factors, narrow_momentum, narrow_gradient]
    mine, theirs = new_factors(place, wide, narrow)
    mine = mine + send_core(theirs)

    pieces = gather_z(hidden)
    block = join(place, pieces)
    mine = mine + send_y(mine, 1) + send_y(mine, 2) + send_y(mine, 3)
    parts = split(after(place, mine), w_out)
    mine = after(mine + send_w(mine), (block, parts))
    blocks = gather_x(block)
    w_kv, post, pre = arrange(after(place, mine), w_key, w_value, post_gain, pre_gain)
    cache_len = after(cache_len, mine)

    frequency = ROPE_BASE ** (-jnp.arange(HD // 2, dtype=F32) * 2.0 / HD)
    position = (cache_len[None, :] + jnp.arange(STEPS)[:, None]).astype(F32)
    angles = position[:, :, None] * frequency
    cosine = jnp.cos(angles)
    sine = jnp.sin(angles)
    cosine = jnp.concatenate([cosine, cosine], axis=-1)
    sine = jnp.concatenate([-sine, sine], axis=-1)

    column = jnp.concatenate(gather_z(mine[:HALF]) + [mine[HALF:]])
    column = after(column, blocks)
    own = jnp.stack(after(gather_x(column), (w_kv, post, pre, cosine, sine)))
    other = send_core(own)

    out_mine = [send_x(after(parts[j], own), -j) for j in range(1, NX)]
    merged_query = merge_query(place, own, other, w_query)

    weights = (merged_query, w_kv, cache_keys, cache_values)
    tables = (post, pre, lengths, cosine, sine)
    start_residual, gathered, *fresh = step(0, 0, ROWS, blocks, None, *tables, [], *weights)
    out_theirs = [send_core(after(v, gathered)) for v in out_mine]
    merged_out = merge_out(place, own, other, parts[0], out_mine, out_theirs)
    residual = [start_residual] * STREAMS
    old = [list(fresh)] * STREAMS
    for turn in range(1, STEPS):
        partial = project(gather_x(gathered), merged_out, BOUNDS)
        attended = []
        for s in range(STREAMS):
            branch = gather_x(add_up(gather_z(partial[s])).astype(BF16))
            residual[s], heads, *fresh = step(
                turn, BOUNDS[s], BOUNDS[s + 1], branch, residual[s], *tables, old[s], *weights
            )
            attended.append(heads)
            old[s] = old[s] + list(fresh)
        gathered = jnp.concatenate(attended)
    (partial,) = project(gather_x(gathered), merged_out, (0, ROWS))
    sums = add_up(gather_z(partial))
    squares = gather_x(jnp.sum(sums * sums, axis=1)[None])
    return finish(place, residual, sums, squares, post)


def solution(mesh):
    rows = P("group", "tensor")
    columns = P(None, "tensor")
    cache = P("group", None, "tensor")
    state = P("group", None, None, "tensor")
    in_specs = (
        rows,
        P("group"),
        P(),
        P(),
        P(),
        columns,
        columns,
        columns,
        P("tensor", None),
        cache,
        cache,
    ) + (state,) * 6
    return jax.shard_map(body, mesh=mesh, in_specs=in_specs, out_specs=rows, check_vma=False)
```
